512 devices in a mesh: seq: 64 (over y, z), dp: 8 (over x, core).
Axes of the slice: x: 4, y: 4, z: 16, core: 2. Of those that a mesh axis runs over, the one named last changes fastest.
Arguments:
- inputs: bfloat16 [8, 8192, 256], P('dp', 'seq'), may hold values from -6 to 6
- cotangent: bfloat16 [8, 8192, 256], P('dp', 'seq'), may hold values from -6 to 6
- filter_taps: float32 [8192, 256], P('seq'), may hold values from -3 to 3
- skip_gain: float32 [256], replicated, may hold values from -1 to 1
Outputs:
- outputs: bfloat16 [8, 8192, 256], P('dp', 'seq')
- filter_grad: float32 [8192, 256], P('seq', 'dp')
The draws below stay inside these ranges and needn't reach their ends.
All inputs are finite; a program needn't handle non-finite values.
Results may differ from the reference program's by a relative error of at most 0.001.
Values sent between devices are 32-bit elements; how exact they have to be, the bound alone decides.
No kernel may reach another device: no remote copies, remote signals or barrier semaphores. Data moves between devices by JAX's collectives and lax.ppermute only.
A program may use at most 64 MiB of HBM per device.

```python
import jax
import jax.numpy as jnp
from jax import lax

CH = 256
LEN = 8192
SAMPLES = 8


def draw_filter_taps(key, part):
    first_key = jax.random.fold_in(key, 0)
    position = jnp.arange(LEN, dtype=jnp.float32)[:, None]
    envelope = 0.5 * lax.rsqrt(position + 1.0)
    values = envelope * jax.random.normal(first_key, (LEN, CH), jnp.float32)
    return jnp.clip(values, -3.0, 3.0)


def steps_of(own_key, dims, shards, least, largest):
    factor_of, own = 1.0, jax.random.fold_in(own_key, 6)
    for dim, shards_of in shards:
        draws = jnp.exp(jax.random.uniform(jax.random.fold_in(own, dim), (shards_of,), jnp.float32, least / len(shards), largest / len(shards)))
        factor_of = factor_of * jnp.repeat(draws, dims[dim] // shards_of).reshape([-1 if axis == dim else 1 for axis in range(len(dims))])
    return factor_of


def normal_values(stream_key, shape, scale, most, cuts=(), kind=jnp.bfloat16):
    result = scale * jax.random.normal(stream_key, shape, jnp.float32)
    if cuts:
        result = result * steps_of(stream_key, shape, cuts, -0.22, 0.18)
    return jnp.clip(result, -most, most).astype(kind)


def setup_inputs(seed: int = 0) -> dict:
    seeds = jax.random.split(jax.random.key(seed), 5)
    return {
        "inputs": normal_values(seeds[0], (SAMPLES, LEN, CH), 1.0, 6.0, ((0, 8), (1, 64))),
        "cotangent": normal_values(seeds[1], (SAMPLES, LEN, CH), 1.0, 6.0, ((0, 8), (1, 64))),
        "filter_taps": draw_filter_taps(jax.random.fold_in(seeds[4], 71), 0),
        "skip_gain": jnp.clip(jax.random.uniform(seeds[3], (CH,), jnp.float32, -1.0, 1.0), -1.0, 1.0),
    }


def reference(inputs, cotangent, filter_taps, skip_gain):
    total = 2 * LEN
    signal = inputs.astype(jnp.float32)
    grads = cotangent.astype(jnp.float32)
    sig_spec = jnp.fft.rfft(signal, n=total, axis=1)
    filt_spec = jnp.fft.rfft(filter_taps, n=total, axis=0)
    conv = jnp.fft.irfft(sig_spec * filt_spec[None], n=total, axis=1)[:, :LEN]
    outputs = (conv + skip_gain * signal).astype(jnp.bfloat16)
    grad_spec = jnp.fft.rfft(grads, n=total, axis=1)
    cross = jnp.sum(grad_spec * jnp.conj(sig_spec), axis=0)
    filter_grad = jnp.fft.irfft(cross, n=total, axis=0)[:LEN]
    return outputs, filter_grad.astype(jnp.float32)
```

```python
import functools
import math

import jax
import jax.numpy as jnp
import ml_dtypes
import numpy as np
from jax import lax
from jax.experimental import pallas as pl
from jax.experimental.pallas import tpu as pltpu
from jax.sharding import PartitionSpec as P

SIDE = 128
HALF = 64
TOTAL = SIDE * SIDE
GROUP = 4
BF = jnp.bfloat16
F32 = jnp.float32


def halves(table):
    high = table.astype(ml_dtypes.bfloat16)
    low = (table - high.astype(np.float64)).astype(ml_dtypes.bfloat16)
    return high, low


def tables():
    blocks = np.arange(HALF)
    places = np.arange(SIDE)
    outer = 2.0 * math.pi * np.outer(np.arange(HALF) + 0.5, blocks) / SIDE
    first = np.concatenate([np.cos(outer), -np.sin(outer)], axis=0)
    high, low = halves(first)
    first_in = np.concatenate([high, low, high, low], axis=1)
    last = first.T * (2.0 / TOTAL)
    high, low = halves(last)
    last_out = np.concatenate([high, high, low], axis=1)
    angle = 2.0 * math.pi * np.outer(np.arange(HALF) + 0.5, places) / TOTAL
    turn = np.stack([np.cos(angle), -np.sin(angle)]).astype(np.float32)
    inner = 2.0 * math.pi * (np.outer(places, places) % SIDE) / SIDE
    cosine, sine = np.cos(inner), np.sin(inner)
    forward = np.block([[cosine, -sine], [sine, cosine]])
    inverse = np.block([[cosine, sine], [-sine, cosine]])
    high, low = halves(forward)
    forward = np.concatenate([high, high, low], axis=0)
    high, low = halves(inverse)
    inverse = np.concatenate([high, high, low], axis=0)
    return first_in, last_out, turn, forward, inverse


def split(value):
    high = value.astype(BF)
    return high, (value - high.astype(F32)).astype(BF)


def dot(left, right):
    return jnp.dot(left, right, preferred_element_type=F32)


def pack_kernel(signal_ref, grads_ref, taps_ref, out_ref):
    for kind, ref in enumerate((signal_ref, grads_ref, taps_ref)):
        turned = ref[...].astype(F32).T
        for sub in range(GROUP):
            rows = turned[HALF * sub : HALF * (sub + 1)]
            out_ref[pl.ds(GROUP * kind + sub, HALF, stride=3 * GROUP), :] = rows


def main_kernel(in_ref, first_ref, last_ref, turn_ref, forward_ref, inverse_ref, out_ref, spread, spectrum, mixed, back):
    stride = 3 * GROUP
    cosine, sine = turn_ref[0], turn_ref[1]

    def load(kind, sub):
        return in_ref[pl.ds(GROUP * kind + sub, HALF, stride=stride), :]

    def place(index, column):
        real, imag = column[:HALF], column[HALF:]
        real, imag = real * cosine - imag * sine, real * sine + imag * cosine
        rows = pl.ds(HALF * index, HALF)
        for part, value in enumerate((real, imag)):
            high, low = split(value)
            spread[rows, pl.ds(SIDE * part, SIDE)] = high
            spread[rows, pl.ds(2 * SIDE + SIDE * part, SIDE)] = low

    for sub in range(GROUP):
        pair = jnp.concatenate([load(0, sub), load(1, sub)], axis=1).astype(BF)
        both = dot(first_ref[:, :SIDE], jnp.concatenate([pair, pair], axis=0))
        place(sub, both[:, :SIDE])
        place(GROUP + sub, both[:, SIDE:])
    for sub in range(0, GROUP, 2):
        pair = jnp.concatenate([load(2, sub), load(2, sub + 1)], axis=1)
        high, low = split(pair)
        both = dot(first_ref[...], jnp.concatenate([high, high, low, low], axis=0))
        place(2 * GROUP + sub, both[:, :SIDE])
        place(2 * GROUP + sub + 1, both[:, SIDE:])

    spectrum[...] = dot(spread[...], forward_ref[: 4 * SIDE]) + dot(
        spread[:, : 2 * SIDE], forward_ref[4 * SIDE :]
    )

    for sub in range(GROUP):
        parts = []
        for kind in range(3):
            rows = pl.ds(HALF * (GROUP * kind + sub), HALF)
            parts.append((spectrum[rows, :SIDE], spectrum[rows, SIDE:]))
        (sig_r, sig_i), (grad_r, grad_i), (filt_r, filt_i) = parts
        products = (
            (sub, sig_r * filt_r - sig_i * filt_i, sig_r * filt_i + sig_i * filt_r),
            (GROUP + sub, grad_r * sig_r + grad_i * sig_i, grad_i * sig_r - grad_r * sig_i),
        )
        for index, real, imag in products:
            rows = pl.ds(HALF * index, HALF)
            for part, value in enumerate((real, imag)):
                high, low = split(value)
                mixed[rows, pl.ds(SIDE * part, SIDE)] = high
                mixed[rows, pl.ds(2 * SIDE + SIDE * part, SIDE)] = low

    back[...] = dot(mixed[...], inverse_ref[: 4 * SIDE]) + dot(
        mixed[:, : 2 * SIDE], inverse_ref[4 * SIDE :]
    )

    for index in range(0, 2 * GROUP, 2):
        stacks = []
        for one in (index, index + 1):
            rows = pl.ds(HALF * one, HALF)
            real, imag = back[rows, :SIDE], back[rows, SIDE:]
            value = jnp.concatenate(
                [real * cosine + imag * sine, imag * cosine - real * sine], axis=0
            )
            high, low = split(value)
            stacks.append(jnp.concatenate([high, low, high], axis=0))
        both = dot(last_ref[...], jnp.concatenate(stacks, axis=1))
        out_ref[pl.ds(index, HALF, stride=2 * GROUP), :] = both[:, :SIDE]
        out_ref[pl.ds(index + 1, HALF, stride=2 * GROUP), :] = both[:, SIDE:]


def pick_kernel(in_ref, out_ref):
    for sub in range(GROUP):
        rows = in_ref[pl.ds(GROUP + sub, HALF, stride=2 * GROUP), :]
        out_ref[pl.ds(HALF * sub, HALF), :] = rows


def finish_kernel(in_ref, signal_ref, gain_ref, out_ref):
    rows = [in_ref[pl.ds(sub, HALF, stride=2 * GROUP), :] for sub in range(GROUP)]
    conv = jnp.concatenate(rows, axis=0).T
    out_ref[...] = (conv + gain_ref[...] * signal_ref[...].astype(F32)).astype(BF)


def sum_kernel(in_ref, out_ref):
    out_ref[...] = jnp.sum(in_ref[...], axis=0).T


def call(kernel, shape, dtype, *args, flops=1000, scratch=()):
    size = math.prod(shape) * jnp.dtype(dtype).itemsize
    size += sum(math.prod(a.shape) * a.dtype.itemsize for a in args)
    return pl.pallas_call(
        kernel,
        out_shape=jax.ShapeDtypeStruct(shape, dtype),
        scratch_shapes=list(scratch),
        cost_estimate=pl.CostEstimate(flops=flops, bytes_accessed=size, transcendentals=0),
        compiler_params=pltpu.CompilerParams(vmem_limit_bytes=24 * 1024 * 1024),
    )(*args)


def body(inputs, cotangent, filter_taps, skip_gain):
    _, rows, chans = inputs.shape
    parts = lax.axis_size("seq")
    shares = lax.axis_size("dp")
    signal = inputs[0]
    packed = call(pack_kernel, (parts * 3 * GROUP, rows), F32, signal, cotangent[0], filter_taps)
    packed = packed.reshape(parts, 3, GROUP, rows)
    columns = lax.all_to_all(packed, "seq", split_axis=0, concat_axis=0, tiled=True)
    columns = columns.reshape(parts * 3 * GROUP, rows)
    wide = 2 * SIDE
    settled = call(
        main_kernel,
        (parts * 2 * GROUP, rows),
        F32,
        columns,
        *[jnp.asarray(t) for t in tables()],
        flops=800_000_000,
        scratch=(
            pltpu.VMEM((3 * GROUP * HALF, 2 * wide), BF),
            pltpu.VMEM((3 * GROUP * HALF, wide), F32),
            pltpu.VMEM((2 * GROUP * HALF, 2 * wide), BF),
            pltpu.VMEM((2 * GROUP * HALF, wide), F32),
        ),
    )
    settled = settled.reshape(parts, 2 * GROUP, rows)
    owned = lax.all_to_all(settled, "seq", split_axis=0, concat_axis=0, tiled=True)
    owned = owned.reshape(parts * 2 * GROUP, rows)
    partial = call(pick_kernel, (chans, rows), F32, owned).reshape(shares, chans // shares, rows)
    partial = lax.all_to_all(partial, "dp", split_axis=0, concat_axis=0, tiled=True)
    outputs = call(finish_kernel, (rows, chans), BF, owned, signal, skip_gain[None])
    filter_grad = call(sum_kernel, (rows, chans // shares), F32, partial)
    return outputs[None], filter_grad


def solution(mesh):
    placed = (P("dp", "seq", None), P("dp", "seq", None), P("seq", None), P())
    return jax.shard_map(
        body,
        mesh=mesh,
        in_specs=placed,
        out_specs=(P("dp", "seq", None), P("seq", "dp")),
        check_vma=False,
    )
```

```python
import functools
import math

import jax
import jax.numpy as jnp
import ml_dtypes
import numpy as np
from jax import lax
from jax.experimental import pallas as pl
from jax.experimental.pallas import tpu as pltpu
from jax.sharding import PartitionSpec as P

SIDE = 128
HALF = 64
TOTAL = SIDE * SIDE
GROUP = 4
BLOCK = 32
SENT = 2 * GROUP + 1
BACK = GROUP + 1
MID = HALF + BLOCK
BF = jnp.bfloat16
F32 = jnp.float32


def halves(table):
    high = table.astype(ml_dtypes.bfloat16)
    low = (table - high.astype(np.float64)).astype(ml_dtypes.bfloat16)
    return high, low


def tables():
    blocks = np.arange(HALF)
    places = np.arange(SIDE)
    outer = 2.0 * math.pi * np.outer(np.arange(HALF) + 0.5, blocks) / SIDE
    first = np.concatenate([np.cos(outer), -np.sin(outer)], axis=0)
    high, low = halves(first)
    first_in = np.concatenate([high, low, high, low], axis=1)
    last = first.T * (2.0 / TOTAL)
    high, low = halves(last)
    last_out = np.concatenate([high, high, low], axis=1)
    angle = 2.0 * math.pi * np.outer(np.arange(HALF) + 0.5, places) / TOTAL
    turn = np.stack([np.cos(angle), -np.sin(angle)]).astype(np.float32)
    inner = 2.0 * math.pi * (np.outer(places, places) % SIDE) / SIDE
    cosine, sine = np.cos(inner), np.sin(inner)
    forward = np.block([[cosine, -sine], [sine, cosine]])
    inverse = np.block([[cosine, sine], [-sine, cosine]])
    high, low = halves(forward)
    forward = np.concatenate([high, high, low], axis=0)
    high, low = halves(inverse)
    inverse = np.concatenate([high, high, low], axis=0)
    return first_in, last_out, turn, forward, inverse


def split(value):
    high = value.astype(BF)
    return high, (value - high.astype(F32)).astype(BF)


def dot(left, right):
    return jnp.dot(left, right, preferred_element_type=F32)


def pack_kernel(own_ref, signal_hbm, grads_hbm, taps_hbm, out_ref, signal_ref, grads_ref, taps_ref, turned, sems):
    pairs = ((signal_hbm, signal_ref), (grads_hbm, grads_ref), (taps_hbm, taps_ref))
    copies = [pltpu.make_async_copy(src, dst, sems.at[i]) for i, (src, dst) in enumerate(pairs)]
    for copy in copies:
        copy.start()
    for kind, ref in enumerate((signal_ref, grads_ref)):
        copies[kind].wait()
        value = ref[...].astype(F32).T
        for block in range(2 * GROUP):
            odd, sub = divmod(block, GROUP)
            rows = value[BLOCK * block : BLOCK * (block + 1)]
            out_ref[pl.ds(SENT * odd + GROUP * kind + sub, BLOCK, stride=2 * SENT), :] = rows
    copies[2].wait()
    turned[...] = taps_ref[...].T
    sub = own_ref[0] // 2
    for odd in range(2):
        start = pl.multiple_of(BLOCK * (GROUP * odd + sub), BLOCK)
        out_ref[pl.ds(SENT * odd + 2 * GROUP, BLOCK, stride=2 * SENT), :] = turned[pl.ds(start, BLOCK), :]


def place(spread, turn_ref, index, column):
    cosine, sine = turn_ref[0], turn_ref[1]
    real, imag = column[:HALF], column[HALF:]
    real, imag = real * cosine - imag * sine, real * sine + imag * cosine
    keep(spread, index, real, imag)


def keep(ref, index, real, imag):
    rows = pl.ds(HALF * index, HALF)
    for part, value in enumerate((real, imag)):
        high, low = split(value)
        ref[rows, pl.ds(SIDE * part, SIDE)] = high
        ref[rows, pl.ds(2 * SIDE + SIDE * part, SIDE)] = low


def wide_dot(ref, table_ref):
    return dot(ref[...], table_ref[: 4 * SIDE]) + dot(ref[:, : 2 * SIDE], table_ref[4 * SIDE :])


def settle(back, last_ref, turn_ref):
    cosine, sine = turn_ref[0], turn_ref[1]
    results = []
    for index in range(0, GROUP, 2):
        stacks = []
        for one in (index, index + 1):
            rows = pl.ds(HALF * one, HALF)
            real, imag = back[rows, :SIDE], back[rows, SIDE:]
            value = jnp.concatenate(
                [real * cosine + imag * sine, imag * cosine - real * sine], axis=0
            )
            high, low = split(value)
            stacks.append(jnp.concatenate([high, low, high], axis=0))
        both = dot(last_ref[...], jnp.concatenate(stacks, axis=1))
        results += [both[:, :SIDE], both[:, SIDE:]]
    return results


def grad_kernel(own_ref, in_ref, first_ref, last_ref, turn_ref, forward_ref, inverse_ref, spec_ref, out_ref, spread, spectrum, mixed, back, taps):
    def load(row):
        return in_ref[pl.ds(row, HALF, stride=SENT), :]

    taps[...] = load(2 * GROUP)
    for sub in range(GROUP):
        pair = jnp.concatenate([load(sub), load(GROUP + sub)], axis=1).astype(BF)
        both = dot(first_ref[:, :SIDE], jnp.concatenate([pair, pair], axis=0))
        place(spread, turn_ref, sub, both[:, :SIDE])
        place(spread, turn_ref, GROUP + sub, both[:, SIDE:])
    spectrum[...] = wide_dot(spread, forward_ref)
    spec_ref[...] = spectrum[: GROUP * HALF]
    for sub in range(GROUP):
        parts = []
        for kind in range(2):
            rows = pl.ds(HALF * (GROUP * kind + sub), HALF)
            parts.append((spectrum[rows, :SIDE], spectrum[rows, SIDE:]))
        (sig_r, sig_i), (grad_r, grad_i) = parts
        keep(mixed, sub, grad_r * sig_r + grad_i * sig_i, grad_i * sig_r - grad_r * sig_i)
    back[...] = wide_dot(mixed, inverse_ref)
    for sub, value in enumerate(settle(back, last_ref, turn_ref)):
        for target in range(sub, 2 * GROUP, GROUP):
            out_ref[pl.ds(MID * target, HALF), :] = value
    start = pl.multiple_of(BLOCK * (own_ref[0] % 2), BLOCK)
    half = taps[pl.ds(start, BLOCK), :]
    for target in range(2 * GROUP):
        out_ref[pl.ds(MID * target + HALF, BLOCK), :] = half


def conv_kernel(in_ref, spec_ref, first_ref, last_ref, turn_ref, forward_ref, inverse_ref, out_ref, spread, spectrum, mixed, back):
    def taps(sub):
        starts = [MID * (2 * sub + core) + HALF for core in range(2)]
        return jnp.concatenate([in_ref[pl.ds(start, BLOCK), :] for start in starts], axis=0)

    for sub in range(0, GROUP, 2):
        high, low = split(jnp.concatenate([taps(sub), taps(sub + 1)], axis=1))
        both = dot(first_ref[...], jnp.concatenate([high, high, low, low], axis=0))
        place(spread, turn_ref, sub, both[:, :SIDE])
        place(spread, turn_ref, sub + 1, both[:, SIDE:])
    spectrum[...] = wide_dot(spread, forward_ref)
    for sub in range(GROUP):
        rows = pl.ds(HALF * sub, HALF)
        sig_r, sig_i = spec_ref[rows, :SIDE], spec_ref[rows, SIDE:]
        filt_r, filt_i = spectrum[rows, :SIDE], spectrum[rows, SIDE:]
        keep(mixed, sub, sig_r * filt_r - sig_i * filt_i, sig_r * filt_i + sig_i * filt_r)
    back[...] = wide_dot(mixed, inverse_ref)
    for sub, value in enumerate(settle(back, last_ref, turn_ref)):
        out_ref[pl.ds(sub, HALF, stride=BACK), :] = value
    total = in_ref[pl.ds(0, HALF), :]
    for source in range(1, 2 * GROUP):
        total = total + in_ref[pl.ds(MID * source, HALF), :]
    out_ref[pl.ds(GROUP, HALF, stride=BACK), :] = total


def finish_kernel(own_ref, in_ref, signal_ref, gain_ref, out_ref, grad_ref):
    def load(odd, row):
        return in_ref[pl.ds(BACK * odd + row, BLOCK, stride=2 * BACK), :]

    conv = jnp.concatenate([load(*divmod(block, GROUP)) for block in range(2 * GROUP)], axis=0)
    out_ref[...] = (conv.T + gain_ref[...] * signal_ref[...].astype(F32)).astype(BF)
    odd = own_ref[0] // GROUP
    grad_ref[...] = jnp.where(odd == 0, load(0, GROUP), load(1, GROUP))


def call(kernel, shapes, *args, flops=1000, scratch=(), hbm=False, scalar=False):
    outs = [jax.ShapeDtypeStruct(*one) for one in shapes]
    size = sum(math.prod(a.shape) * a.dtype.itemsize for a in [*args, *outs])
    vmem = pl.BlockSpec(memory_space=pltpu.VMEM)
    place_in = pl.BlockSpec(memory_space=pltpu.HBM) if hbm else vmem
    specs = [place_in] * len(args)
    if scalar:
        specs[0] = pl.BlockSpec(memory_space=pltpu.SMEM)
    result = pl.pallas_call(
        kernel,
        out_shape=outs,
        in_specs=specs,
        out_specs=[vmem] * len(outs),
        scratch_shapes=list(scratch),
        cost_estimate=pl.CostEstimate(flops=flops, bytes_accessed=size, transcendentals=0),
        compiler_params=pltpu.CompilerParams(vmem_limit_bytes=58000000 if hbm else 24 * 1024 * 1024),
    )(*args)
    return result if len(shapes) > 1 else result[0]


def exchange(rows, axis, inner):
    parts = lax.axis_size(axis)
    blocks = rows.reshape((parts, *inner, rows.shape[-1]))
    return lax.all_to_all(blocks, axis, split_axis=0, concat_axis=0, tiled=True).reshape(rows.shape)


def body(inputs, cotangent, filter_taps, skip_gain):
    _, rows, chans = inputs.shape
    parts, shares = lax.axis_size("seq"), lax.axis_size("dp")
    own = lax.axis_index("dp").astype(jnp.int32)[None]
    signal = inputs[0]
    wide = 2 * SIDE
    constants = [jnp.asarray(t) for t in tables()]

    def room(count):
        return (
            pltpu.VMEM((count * GROUP * HALF, 2 * wide), BF),
            pltpu.VMEM((count * GROUP * HALF, wide), F32),
            pltpu.VMEM((GROUP * HALF, 2 * wide), BF),
            pltpu.VMEM((GROUP * HALF, wide), F32),
        )

    packed = call(
        pack_kernel,
        [((SENT * parts, rows), F32)],
        own,
        signal,
        cotangent[0],
        filter_taps,
        hbm=True,
        scalar=True,
        scratch=(
            pltpu.VMEM((rows, chans), BF),
            pltpu.VMEM((rows, chans), BF),
            pltpu.VMEM((rows, chans), F32),
            pltpu.VMEM((chans, rows), F32),
            pltpu.SemaphoreType.DMA((3,)),
        ),
    )
    columns = exchange(packed, "seq", (SENT, 1))
    spec, partial = call(
        grad_kernel,
        [((GROUP * HALF, wide), F32), ((MID * shares, rows), F32)],
        own,
        columns,
        *constants,
        flops=500_000_000,
        scalar=True,
        scratch=(*room(2), pltpu.VMEM((HALF, rows), F32)),
    )
    partial = exchange(partial, "dp", (MID,))
    settled = call(
        conv_kernel,
        [((BACK * parts, rows), F32)],
        partial,
        spec,
        *constants,
        flops=500_000_000,
        scratch=room(1),
    )
    settled = exchange(settled, "seq", (BACK, 1))
    outputs, filter_grad = call(
        finish_kernel,
        [((rows, chans), BF), ((chans // shares, rows), F32)],
        own,
        settled,
        signal,
        skip_gain[None],
        scalar=True,
    )
    return outputs[None], filter_grad.T


def solution(mesh):
    placed = (P("dp", "seq", None), P("dp", "seq", None), P("seq", None), P())
    return jax.shard_map(
        body,
        mesh=mesh,
        in_specs=placed,
        out_specs=(P("dp", "seq", None), P("seq", "dp")),
        check_vma=False,
    )
```

```python
import functools
import math

import jax
import jax.numpy as jnp
import ml_dtypes
import numpy as np
from jax import lax
from jax.experimental import pallas as pl
from jax.experimental.pallas import tpu as pltpu
from jax.sharding import PartitionSpec as P

SIDE = 128
HALF = 64
TOTAL = SIDE * SIDE
GROUP = 4
BLOCK = 32
SENT = 2 * GROUP + 1
BACK = GROUP + 1
MID = HALF + BLOCK
BF = jnp.bfloat16
F32 = jnp.float32


def halves(table):
    high = table.astype(ml_dtypes.bfloat16)
    low = (table - high.astype(np.float64)).astype(ml_dtypes.bfloat16)
    return high, low


def tables():
    blocks = np.arange(HALF)
    places = np.arange(SIDE)
    outer = 2.0 * math.pi * np.outer(np.arange(HALF) + 0.5, blocks) / SIDE
    first = np.concatenate([np.cos(outer), -np.sin(outer)], axis=0)
    high, low = halves(first)
    first_in = np.concatenate([high, low, high, low], axis=1)
    last = first.T * (2.0 / TOTAL)
    high, low = halves(last)
    last_out = np.concatenate([high, high, low], axis=1)
    angle = 2.0 * math.pi * np.outer(np.arange(HALF) + 0.5, places) / TOTAL
    turn = np.stack([np.cos(angle), -np.sin(angle)]).astype(np.float32)
    inner = 2.0 * math.pi * (np.outer(places, places) % SIDE) / SIDE
    cosine, sine = np.cos(inner), np.sin(inner)
    forward = np.block([[cosine, -sine], [sine, cosine]])
    inverse = np.block([[cosine, sine], [-sine, cosine]])
    high, low = halves(forward)
    forward = np.concatenate([high, high, low], axis=0)
    high, low = halves(inverse)
    inverse = np.concatenate([high, high, low], axis=0)
    return first_in, last_out, turn, forward, inverse


def split(value):
    high = value.astype(BF)
    return high, (value - high.astype(F32)).astype(BF)


def dot(left, right):
    return jnp.dot(left, right, preferred_element_type=F32)


def pack_kernel(own_ref, seat_ref, signal_hbm, grads_hbm, taps_hbm, gain_hbm, out_ref, signal_ref, grads_ref, taps_ref, gain_ref, turned, sems):
    pairs = ((signal_hbm, signal_ref), (grads_hbm, grads_ref), (taps_hbm, taps_ref), (gain_hbm, gain_ref))
    copies = [pltpu.make_async_copy(src, dst, sems.at[i]) for i, (src, dst) in enumerate(pairs)]
    for copy in copies:
        copy.start()
    for kind, ref in enumerate((signal_ref, grads_ref)):
        copies[kind].wait()
        value = ref[...].astype(F32).T
        for block in range(2 * GROUP):
            odd, sub = divmod(block, GROUP)
            rows = value[BLOCK * block : BLOCK * (block + 1)]
            out_ref[pl.ds(SENT * odd + GROUP * kind + sub, BLOCK, stride=2 * SENT), :] = rows
    copies[2].wait()
    copies[3].wait()

    @pl.when(seat_ref[0] == 0)
    def _():
        taps_ref[:1] = taps_ref[:1] + gain_ref[...]

    turned[...] = taps_ref[...].T
    sub = own_ref[0] // 2
    for odd in range(2):
        start = pl.multiple_of(BLOCK * (GROUP * odd + sub), BLOCK)
        out_ref[pl.ds(SENT * odd + 2 * GROUP, BLOCK, stride=2 * SENT), :] = turned[pl.ds(start, BLOCK), :]


def place(spread, turn_ref, index, column):
    cosine, sine = turn_ref[0], turn_ref[1]
    real, imag = column[:HALF], column[HALF:]
    real, imag = real * cosine - imag * sine, real * sine + imag * cosine
    keep(spread, index, real, imag)


def keep(ref, index, real, imag):
    rows = pl.ds(HALF * index, HALF)
    for part, value in enumerate((real, imag)):
        high, low = split(value)
        ref[rows, pl.ds(SIDE * part, SIDE)] = high
        ref[rows, pl.ds(2 * SIDE + SIDE * part, SIDE)] = low


def wide_dot(ref, table_ref):
    return dot(ref[...], table_ref[: 4 * SIDE]) + dot(ref[:, : 2 * SIDE], table_ref[4 * SIDE :])


def settle(back, last_ref, turn_ref):
    cosine, sine = turn_ref[0], turn_ref[1]
    results = []
    for index in range(0, GROUP, 2):
        stacks = []
        for one in (index, index + 1):
            rows = pl.ds(HALF * one, HALF)
            real, imag = back[rows, :SIDE], back[rows, SIDE:]
            value = jnp.concatenate(
                [real * cosine + imag * sine, imag * cosine - real * sine], axis=0
            )
            high, low = split(value)
            stacks.append(jnp.concatenate([high, low, high], axis=0))
        both = dot(last_ref[...], jnp.concatenate(stacks, axis=1))
        results += [both[:, :SIDE], both[:, SIDE:]]
    return results


def grad_kernel(own_ref, in_ref, first_ref, last_ref, turn_ref, forward_ref, inverse_ref, spec_ref, out_ref, spread, spectrum, mixed, back, taps):
    def load(row):
        return in_ref[pl.ds(row, HALF, stride=SENT), :]

    taps[...] = load(2 * GROUP)
    for sub in range(GROUP):
        pair = jnp.concatenate([load(sub), load(GROUP + sub)], axis=1).astype(BF)
        both = dot(first_ref[:, :SIDE], jnp.concatenate([pair, pair], axis=0))
        place(spread, turn_ref, sub, both[:, :SIDE])
        place(spread, turn_ref, GROUP + sub, both[:, SIDE:])
    spectrum[...] = wide_dot(spread, forward_ref)
    spec_ref[...] = spectrum[: GROUP * HALF]
    for sub in range(GROUP):
        parts = []
        for kind in range(2):
            rows = pl.ds(HALF * (GROUP * kind + sub), HALF)
            parts.append((spectrum[rows, :SIDE], spectrum[rows, SIDE:]))
        (sig_r, sig_i), (grad_r, grad_i) = parts
        keep(mixed, sub, grad_r * sig_r + grad_i * sig_i, grad_i * sig_r - grad_r * sig_i)
    back[...] = wide_dot(mixed, inverse_ref)
    for sub, value in enumerate(settle(back, last_ref, turn_ref)):
        for target in range(sub, 2 * GROUP, GROUP):
            out_ref[pl.ds(MID * target, HALF), :] = value
    start = pl.multiple_of(BLOCK * (own_ref[0] % 2), BLOCK)
    half = taps[pl.ds(start, BLOCK), :]
    for target in range(2 * GROUP):
        out_ref[pl.ds(MID * target + HALF, BLOCK), :] = half


def conv_kernel(in_ref, spec_ref, first_ref, last_ref, turn_ref, forward_ref, inverse_ref, out_ref, spread, spectrum, mixed, back):
    def taps(sub):
        starts = [MID * (2 * sub + core) + HALF for core in range(2)]
        return jnp.concatenate([in_ref[pl.ds(start, BLOCK), :] for start in starts], axis=0)

    for sub in range(0, GROUP, 2):
        high, low = split(jnp.concatenate([taps(sub), taps(sub + 1)], axis=1))
        both = dot(first_ref[...], jnp.concatenate([high, high, low, low], axis=0))
        place(spread, turn_ref, sub, both[:, :SIDE])
        place(spread, turn_ref, sub + 1, both[:, SIDE:])
    spectrum[...] = wide_dot(spread, forward_ref)
    for sub in range(GROUP):
        rows = pl.ds(HALF * sub, HALF)
        sig_r, sig_i = spec_ref[rows, :SIDE], spec_ref[rows, SIDE:]
        filt_r, filt_i = spectrum[rows, :SIDE], spectrum[rows, SIDE:]
        keep(mixed, sub, sig_r * filt_r - sig_i * filt_i, sig_r * filt_i + sig_i * filt_r)
    back[...] = wide_dot(mixed, inverse_ref)
    for sub, value in enumerate(settle(back, last_ref, turn_ref)):
        out_ref[pl.ds(sub, HALF, stride=BACK), :] = value
    total = in_ref[pl.ds(0, HALF), :]
    for source in range(1, 2 * GROUP):
        total = total + in_ref[pl.ds(MID * source, HALF), :]
    out_ref[pl.ds(GROUP, HALF, stride=BACK), :] = total


def finish_kernel(own_ref, in_ref, out_ref, grad_ref):
    def load(odd, row):
        return in_ref[pl.ds(BACK * odd + row, BLOCK, stride=2 * BACK), :]

    conv = jnp.concatenate([load(*divmod(block, GROUP)) for block in range(2 * GROUP)], axis=0)
    out_ref[...] = conv.T.astype(BF)
    odd = own_ref[0] // GROUP
    grad_ref[...] = jnp.where(odd == 0, load(0, GROUP), load(1, GROUP))


def call(kernel, shapes, *args, flops=1000, scratch=(), hbm=False, scalars=0):
    outs = [jax.ShapeDtypeStruct(*one) for one in shapes]
    size = sum(math.prod(a.shape) * a.dtype.itemsize for a in [*args, *outs])
    vmem = pl.BlockSpec(memory_space=pltpu.VMEM)
    place_in = pl.BlockSpec(memory_space=pltpu.HBM) if hbm else vmem
    specs = [place_in] * len(args)
    specs[:scalars] = [pl.BlockSpec(memory_space=pltpu.SMEM)] * scalars
    result = pl.pallas_call(
        kernel,
        out_shape=outs,
        in_specs=specs,
        out_specs=[vmem] * len(outs),
        scratch_shapes=list(scratch),
        cost_estimate=pl.CostEstimate(flops=flops, bytes_accessed=size, transcendentals=0),
        compiler_params=pltpu.CompilerParams(vmem_limit_bytes=58000000 if hbm else 24 * 1024 * 1024),
    )(*args)
    return result if len(shapes) > 1 else result[0]


def exchange(rows, axis, inner):
    parts = lax.axis_size(axis)
    blocks = rows.reshape((parts, *inner, rows.shape[-1]))
    return lax.all_to_all(blocks, axis, split_axis=0, concat_axis=0, tiled=True).reshape(rows.shape)


def body(inputs, cotangent, filter_taps, skip_gain):
    _, rows, chans = inputs.shape
    parts, shares = lax.axis_size("seq"), lax.axis_size("dp")
    own = lax.axis_index("dp").astype(jnp.int32)[None]
    seat = lax.axis_index("seq").astype(jnp.int32)[None]
    wide = 2 * SIDE
    constants = [jnp.asarray(t) for t in tables()]

    def room(count):
        return (
            pltpu.VMEM((count * GROUP * HALF, 2 * wide), BF),
            pltpu.VMEM((count * GROUP * HALF, wide), F32),
            pltpu.VMEM((GROUP * HALF, 2 * wide), BF),
            pltpu.VMEM((GROUP * HALF, wide), F32),
        )

    packed = call(
        pack_kernel,
        [((SENT * parts, rows), F32)],
        own,
        seat,
        inputs[0],
        cotangent[0],
        filter_taps,
        skip_gain[None],
        hbm=True,
        scalars=2,
        scratch=(
            pltpu.VMEM((rows, chans), BF),
            pltpu.VMEM((rows, chans), BF),
            pltpu.VMEM((rows, chans), F32),
            pltpu.VMEM((1, chans), F32),
            pltpu.VMEM((chans, rows), F32),
            pltpu.SemaphoreType.DMA((4,)),
        ),
    )
    columns = exchange(packed, "seq", (SENT, 1))
    spec, partial = call(
        grad_kernel,
        [((GROUP * HALF, wide), F32), ((MID * shares, rows), F32)],
        own,
        columns,
        *constants,
        flops=500_000_000,
        scalars=1,
        scratch=(*room(2), pltpu.VMEM((HALF, rows), F32)),
    )
    partial = exchange(partial, "dp", (MID,))
    settled = call(
        conv_kernel,
        [((BACK * parts, rows), F32)],
        partial,
        spec,
        *constants,
        flops=500_000_000,
        scratch=room(1),
    )
    settled = exchange(settled, "seq", (BACK, 1))
    outputs, filter_grad = call(
        finish_kernel,
        [((rows, chans), BF), ((chans // shares, rows), F32)],
        own,
        settled,
        scalars=1,
    )
    return outputs[None], filter_grad.T


def solution(mesh):
    placed = (P("dp", "seq", None), P("dp", "seq", None), P("seq", None), P())
    return jax.shard_map(
        body,
        mesh=mesh,
        in_specs=placed,
        out_specs=(P("dp", "seq", None), P("seq", "dp")),
        check_vma=False,
    )
```

```python
import functools
import math

import jax
import jax.numpy as jnp
import ml_dtypes
import numpy as np
from jax import lax
from jax.experimental import pallas as pl
from jax.experimental.pallas import tpu as pltpu
from jax.sharding import PartitionSpec as P

SIDE = 128
HALF = 64
TOTAL = SIDE * SIDE
GROUP = 4
BLOCK = 32
SENT = 2 * GROUP + 1
BACK = GROUP + 1
MID = 2 * HALF
BF = jnp.bfloat16
F32 = jnp.float32


def halves(table):
    high = table.astype(ml_dtypes.bfloat16)
    low = (table - high.astype(np.float64)).astype(ml_dtypes.bfloat16)
    return high, low


def tables():
    blocks = np.arange(HALF)
    places = np.arange(SIDE)
    outer = 2.0 * math.pi * np.outer(np.arange(HALF) + 0.5, blocks) / SIDE
    first = np.concatenate([np.cos(outer), -np.sin(outer)], axis=0)
    high, low = halves(first)
    first_in = np.concatenate([high, low, high, low], axis=1)
    last = first.T * (2.0 / TOTAL)
    high, low = halves(last)
    last_out = np.concatenate([high, high, low], axis=1)
    angle = 2.0 * math.pi * np.outer(np.arange(HALF) + 0.5, places) / TOTAL
    turn = np.stack([np.cos(angle), -np.sin(angle)]).astype(np.float32)
    inner = 2.0 * math.pi * (np.outer(places, places) % SIDE) / SIDE
    cosine, sine = np.cos(inner), np.sin(inner)
    forward = np.block([[cosine, -sine], [sine, cosine]])
    inverse = np.block([[cosine, sine], [-sine, cosine]])
    high, low = halves(forward)
    forward = np.concatenate([high, high, low], axis=0)
    high, low = halves(inverse)
    inverse = np.concatenate([high, high, low], axis=0)
    return first_in, last_out, turn, forward, inverse


def split(value):
    high = value.astype(BF)
    return high, (value - high.astype(F32)).astype(BF)


def dot(left, right):
    return jnp.dot(left, right, preferred_element_type=F32)


def pack_kernel(own_ref, seat_ref, signal_hbm, grads_hbm, taps_hbm, gain_hbm, out_ref, signal_ref, grads_ref, taps_ref, gain_ref, turned, sems):
    pairs = ((signal_hbm, signal_ref), (grads_hbm, grads_ref), (taps_hbm, taps_ref), (gain_hbm, gain_ref))
    copies = [pltpu.make_async_copy(src, dst, sems.at[i]) for i, (src, dst) in enumerate(pairs)]
    for copy in copies:
        copy.start()
    for kind, ref in enumerate((signal_ref, grads_ref)):
        copies[kind].wait()
        value = ref[...].astype(F32).T
        for sub in range(GROUP):
            rows = value[HALF * sub : HALF * (sub + 1)]
            out_ref[pl.ds(GROUP * kind + sub, HALF, stride=SENT), :] = rows
    copies[2].wait()
    copies[3].wait()

    @pl.when(seat_ref[0] == 0)
    def _():
        taps_ref[:1] = taps_ref[:1] + gain_ref[...]

    turned[...] = taps_ref[...].T
    start = pl.multiple_of(HALF * (own_ref[0] // 2), HALF)
    out_ref[pl.ds(2 * GROUP, HALF, stride=SENT), :] = turned[pl.ds(start, HALF), :]


def place(spread, turn_ref, index, column):
    cosine, sine = turn_ref[0], turn_ref[1]
    real, imag = column[:HALF], column[HALF:]
    real, imag = real * cosine - imag * sine, real * sine + imag * cosine
    keep(spread, index, real, imag)


def keep(ref, index, real, imag):
    rows = pl.ds(HALF * index, HALF)
    for part, value in enumerate((real, imag)):
        high, low = split(value)
        ref[rows, pl.ds(SIDE * part, SIDE)] = high
        ref[rows, pl.ds(2 * SIDE + SIDE * part, SIDE)] = low


def wide_dot(ref, table_ref):
    return dot(ref[...], table_ref[: 4 * SIDE]) + dot(ref[:, : 2 * SIDE], table_ref[4 * SIDE :])


def settle(back, last_ref, turn_ref):
    cosine, sine = turn_ref[0], turn_ref[1]
    results = []
    for index in range(0, GROUP, 2):
        stacks = []
        for one in (index, index + 1):
            rows = pl.ds(HALF * one, HALF)
            real, imag = back[rows, :SIDE], back[rows, SIDE:]
            value = jnp.concatenate(
                [real * cosine + imag * sine, imag * cosine - real * sine], axis=0
            )
            high, low = split(value)
            stacks.append(jnp.concatenate([high, low, high], axis=0))
        both = dot(last_ref[...], jnp.concatenate(stacks, axis=1))
        results += [both[:, :SIDE], both[:, SIDE:]]
    return results


def grad_kernel(in_ref, first_ref, last_ref, turn_ref, forward_ref, inverse_ref, spec_ref, out_ref, spread, spectrum, mixed, back):
    def load(row):
        return in_ref[pl.ds(row, HALF, stride=SENT), :]

    taps = load(2 * GROUP)
    for target in range(GROUP):
        out_ref[pl.ds(MID * target + HALF, HALF), :] = taps
    for sub in range(GROUP):
        pair = jnp.concatenate([load(sub), load(GROUP + sub)], axis=1).astype(BF)
        both = dot(first_ref[:, :SIDE], jnp.concatenate([pair, pair], axis=0))
        place(spread, turn_ref, sub, both[:, :SIDE])
        place(spread, turn_ref, GROUP + sub, both[:, SIDE:])
    spectrum[...] = wide_dot(spread, forward_ref)
    spec_ref[...] = spectrum[: GROUP * HALF]
    for sub in range(GROUP):
        parts = []
        for kind in range(2):
            rows = pl.ds(HALF * (GROUP * kind + sub), HALF)
            parts.append((spectrum[rows, :SIDE], spectrum[rows, SIDE:]))
        (sig_r, sig_i), (grad_r, grad_i) = parts
        keep(mixed, sub, grad_r * sig_r + grad_i * sig_i, grad_i * sig_r - grad_r * sig_i)
    back[...] = wide_dot(mixed, inverse_ref)
    for sub, value in enumerate(settle(back, last_ref, turn_ref)):
        out_ref[pl.ds(MID * sub, HALF), :] = value


def conv_kernel(in_ref, spec_ref, first_ref, last_ref, turn_ref, forward_ref, inverse_ref, out_ref, spread, spectrum, mixed, back):
    def taps(sub):
        return in_ref[pl.ds(MID * sub + HALF, HALF), :]

    for sub in range(0, GROUP, 2):
        high, low = split(jnp.concatenate([taps(sub), taps(sub + 1)], axis=1))
        both = dot(first_ref[...], jnp.concatenate([high, high, low, low], axis=0))
        place(spread, turn_ref, sub, both[:, :SIDE])
        place(spread, turn_ref, sub + 1, both[:, SIDE:])
    spectrum[...] = wide_dot(spread, forward_ref)
    for sub in range(GROUP):
        rows = pl.ds(HALF * sub, HALF)
        sig_r, sig_i = spec_ref[rows, :SIDE], spec_ref[rows, SIDE:]
        filt_r, filt_i = spectrum[rows, :SIDE], spectrum[rows, SIDE:]
        keep(mixed, sub, sig_r * filt_r - sig_i * filt_i, sig_r * filt_i + sig_i * filt_r)
    back[...] = wide_dot(mixed, inverse_ref)
    for sub, value in enumerate(settle(back, last_ref, turn_ref)):
        out_ref[pl.ds(sub, HALF, stride=BACK), :] = value
    total = in_ref[pl.ds(0, HALF), :]
    for source in range(1, GROUP):
        total = total + in_ref[pl.ds(MID * source, HALF), :]
    out_ref[pl.ds(GROUP, HALF, stride=BACK), :] = total


def part_kernel(own_ref, in_ref, send_ref, keep_ref):
    low, high = [in_ref[pl.ds(BACK * BLOCK * half + GROUP, BLOCK, stride=BACK), :] for half in range(2)]
    first = own_ref[0] % 2 == 0
    send_ref[...] = jnp.where(first, high, low)
    keep_ref[...] = jnp.where(first, low, high)


def finish_kernel(in_ref, out_ref):
    rows = [in_ref[pl.ds(sub, HALF, stride=BACK), :] for sub in range(GROUP)]
    out_ref[...] = jnp.concatenate(rows, axis=0).T.astype(BF)


def call(kernel, shapes, *args, flops=1000, scratch=(), hbm=False, scalars=0):
    outs = [jax.ShapeDtypeStruct(*one) for one in shapes]
    size = sum(math.prod(a.shape) * a.dtype.itemsize for a in [*args, *outs])
    vmem = pl.BlockSpec(memory_space=pltpu.VMEM)
    place_in = pl.BlockSpec(memory_space=pltpu.HBM) if hbm else vmem
    specs = [place_in] * len(args)
    specs[:scalars] = [pl.BlockSpec(memory_space=pltpu.SMEM)] * scalars
    result = pl.pallas_call(
        kernel,
        out_shape=outs,
        in_specs=specs,
        out_specs=[vmem] * len(outs),
        scratch_shapes=list(scratch),
        cost_estimate=pl.CostEstimate(flops=flops, bytes_accessed=size, transcendentals=0),
        compiler_params=pltpu.CompilerParams(vmem_limit_bytes=58000000 if hbm else 24 * 1024 * 1024),
    )(*args)
    return result if len(shapes) > 1 else result[0]


def exchange(rows, axis, inner, groups=None):
    parts = len(groups[0]) if groups else lax.axis_size(axis)
    blocks = rows.reshape((parts, *inner, rows.shape[-1]))
    return lax.all_to_all(blocks, axis, split_axis=0, concat_axis=0, tiled=True, axis_index_groups=groups).reshape(rows.shape)


def body(inputs, cotangent, filter_taps, skip_gain):
    _, rows, chans = inputs.shape
    parts, shares = lax.axis_size("seq"), lax.axis_size("dp")
    own = lax.axis_index("dp").astype(jnp.int32)[None]
    seat = lax.axis_index("seq").astype(jnp.int32)[None]
    wide = 2 * SIDE
    constants = [jnp.asarray(t) for t in tables()]

    def room(count):
        return (
            pltpu.VMEM((count * GROUP * HALF, 2 * wide), BF),
            pltpu.VMEM((count * GROUP * HALF, wide), F32),
            pltpu.VMEM((GROUP * HALF, 2 * wide), BF),
            pltpu.VMEM((GROUP * HALF, wide), F32),
        )

    packed = call(
        pack_kernel,
        [((SENT * parts, rows), F32)],
        own,
        seat,
        inputs[0],
        cotangent[0],
        filter_taps,
        skip_gain[None],
        hbm=True,
        scalars=2,
        scratch=(
            pltpu.VMEM((rows, chans), BF),
            pltpu.VMEM((rows, chans), BF),
            pltpu.VMEM((rows, chans), F32),
            pltpu.VMEM((1, chans), F32),
            pltpu.VMEM((chans, rows), F32),
            pltpu.SemaphoreType.DMA((4,)),
        ),
    )
    columns = exchange(packed, "seq", (SENT, 1))
    spec, partial = call(
        grad_kernel,
        [((GROUP * HALF, wide), F32), ((MID * GROUP, rows), F32)],
        columns,
        *constants,
        flops=500_000_000,
        scratch=room(2),
    )
    groups = [list(range(core, shares, 2)) for core in range(2)]
    partial = exchange(partial, "dp", (MID,), groups)
    settled = call(
        conv_kernel,
        [((BACK * parts, rows), F32)],
        partial,
        spec,
        *constants,
        flops=500_000_000,
        scratch=room(1),
    )
    settled = exchange(settled, "seq", (BACK, 1))
    shape = ((chans // shares, rows), F32)
    send, held = call(part_kernel, [shape, shape], own, settled, scalars=1)
    got = lax.ppermute(send, "dp", [(one, one ^ 1) for one in range(shares)])
    outputs = call(finish_kernel, [((rows, chans), BF)], settled, flops=500_000_000)
    filter_grad = held + got
    return outputs[None], filter_grad.T


def solution(mesh):
    placed = (P("dp", "seq", None), P("dp", "seq", None), P("seq", None), P())
    return jax.shard_map(
        body,
        mesh=mesh,
        in_specs=placed,
        out_specs=(P("dp", "seq", None), P("seq", "dp")),
        check_vma=False,
    )
```

```python
import functools
import math

import jax
import jax.numpy as jnp
import ml_dtypes
import numpy as np
from jax import lax
from jax.experimental import pallas as pl
from jax.experimental.pallas import tpu as pltpu
from jax.sharding import PartitionSpec as P

SIDE = 128
HALF = 64
TOTAL = SIDE * SIDE
GROUP = 4
BLOCK = 32
SENT = 2 * GROUP + 1
BACK = GROUP + 1
MID = HALF + BLOCK
BF = jnp.bfloat16
F32 = jnp.float32


def halves(table):
    high = table.astype(ml_dtypes.bfloat16)
    low = (table - high.astype(np.float64)).astype(ml_dtypes.bfloat16)
    return high, low


def tables():
    blocks = np.arange(HALF)
    places = np.arange(SIDE)
    outer = 2.0 * math.pi * np.outer(np.arange(HALF) + 0.5, blocks) / SIDE
    first = np.concatenate([np.cos(outer), -np.sin(outer)], axis=0)
    high, low = halves(first)
    first_in = np.concatenate([high, low, high, low], axis=1)
    last = first.T * (2.0 / TOTAL)
    high, low = halves(last)
    last_out = np.concatenate([high, high, low], axis=1)
    angle = 2.0 * math.pi * np.outer(np.arange(HALF) + 0.5, places) / TOTAL
    turn = np.stack([np.cos(angle), -np.sin(angle)]).astype(np.float32)
    inner = 2.0 * math.pi * (np.outer(places, places) % SIDE) / SIDE
    cosine, sine = np.cos(inner), np.sin(inner)
    forward = np.block([[cosine, -sine], [sine, cosine]])
    inverse = np.block([[cosine, sine], [-sine, cosine]])
    high, low = halves(forward)
    forward = np.concatenate([high, high, low], axis=0)
    high, low = halves(inverse)
    inverse = np.concatenate([high, high, low], axis=0)
    return first_in, last_out, turn, forward, inverse


def split(value):
    high = value.astype(BF)
    return high, (value - high.astype(F32)).astype(BF)


def dot(left, right):
    return jnp.dot(left, right, preferred_element_type=F32)


def mask_kernel(seat_ref, out_ref):
    out_ref[...] = jnp.where(seat_ref[0] == 0, jnp.ones(out_ref.shape, F32), jnp.zeros(out_ref.shape, F32))


def pack_kernel(own_ref, mask_ref, signal_ref, grads_ref, taps_ref, gain_ref, out_ref, turned):
    for kind, ref in enumerate((signal_ref, grads_ref)):
        value = ref[...].astype(F32).T
        for block in range(2 * GROUP):
            odd, sub = divmod(block, GROUP)
            rows = value[BLOCK * block : BLOCK * (block + 1)]
            out_ref[pl.ds(SENT * odd + GROUP * kind + sub, BLOCK, stride=2 * SENT), :] = rows
    taps = taps_ref[...]
    first = lax.broadcasted_iota(jnp.int32, taps.shape, 0) == 0
    taps = taps + jnp.where(first, gain_ref[...] * mask_ref[...], 0.0)
    turned[...] = taps.T
    sub = own_ref[0] // 2
    for odd in range(2):
        start = pl.multiple_of(BLOCK * (GROUP * odd + sub), BLOCK)
        out_ref[pl.ds(SENT * odd + 2 * GROUP, BLOCK, stride=2 * SENT), :] = turned[pl.ds(start, BLOCK), :]


def place(spread, turn_ref, index, column):
    cosine, sine = turn_ref[0], turn_ref[1]
    real, imag = column[:HALF], column[HALF:]
    real, imag = real * cosine - imag * sine, real * sine + imag * cosine
    keep(spread, index, real, imag)


def keep(ref, index, real, imag):
    rows = pl.ds(HALF * index, HALF)
    for part, value in enumerate((real, imag)):
        high, low = split(value)
        ref[rows, pl.ds(SIDE * part, SIDE)] = high
        ref[rows, pl.ds(2 * SIDE + SIDE * part, SIDE)] = low


def wide_dot(ref, table_ref):
    return dot(ref[...], table_ref[: 4 * SIDE]) + dot(ref[:, : 2 * SIDE], table_ref[4 * SIDE :])


def settle(back, last_ref, turn_ref):
    cosine, sine = turn_ref[0], turn_ref[1]
    results = []
    for index in range(0, GROUP, 2):
        stacks = []
        for one in (index, index + 1):
            rows = pl.ds(HALF * one, HALF)
            real, imag = back[rows, :SIDE], back[rows, SIDE:]
            value = jnp.concatenate(
                [real * cosine + imag * sine, imag * cosine - real * sine], axis=0
            )
            high, low = split(value)
            stacks.append(jnp.concatenate([high, low, high], axis=0))
        both = dot(last_ref[...], jnp.concatenate(stacks, axis=1))
        results += [both[:, :SIDE], both[:, SIDE:]]
    return results


def grad_kernel(own_ref, in_ref, first_ref, last_ref, turn_ref, forward_ref, inverse_ref, spec_ref, out_ref, spread, spectrum, mixed, back, taps):
    def load(row):
        return in_ref[pl.ds(row, HALF, stride=SENT), :]

    taps[...] = load(2 * GROUP)
    for sub in range(GROUP):
        pair = jnp.concatenate([load(sub), load(GROUP + sub)], axis=1).astype(BF)
        both = dot(first_ref[:, :SIDE], jnp.concatenate([pair, pair], axis=0))
        place(spread, turn_ref, sub, both[:, :SIDE])
        place(spread, turn_ref, GROUP + sub, both[:, SIDE:])
    spectrum[...] = wide_dot(spread, forward_ref)
    spec_ref[...] = spectrum[: GROUP * HALF]
    for sub in range(GROUP):
        parts = []
        for kind in range(2):
            rows = pl.ds(HALF * (GROUP * kind + sub), HALF)
            parts.append((spectrum[rows, :SIDE], spectrum[rows, SIDE:]))
        (sig_r, sig_i), (grad_r, grad_i) = parts
        keep(mixed, sub, grad_r * sig_r + grad_i * sig_i, grad_i * sig_r - grad_r * sig_i)
    back[...] = wide_dot(mixed, inverse_ref)
    for sub, value in enumerate(settle(back, last_ref, turn_ref)):
        for target in range(sub, 2 * GROUP, GROUP):
            out_ref[pl.ds(MID * target, HALF), :] = value
    start = pl.multiple_of(BLOCK * (own_ref[0] % 2), BLOCK)
    half = taps[pl.ds(start, BLOCK), :]
    for target in range(2 * GROUP):
        out_ref[pl.ds(MID * target + HALF, BLOCK), :] = half


def conv_kernel(in_ref, spec_ref, first_ref, last_ref, turn_ref, forward_ref, inverse_ref, out_ref, spread, spectrum, mixed, back):
    def taps(sub):
        starts = [MID * (2 * sub + core) + HALF for core in range(2)]
        return jnp.concatenate([in_ref[pl.ds(start, BLOCK), :] for start in starts], axis=0)

    for sub in range(0, GROUP, 2):
        high, low = split(jnp.concatenate([taps(sub), taps(sub + 1)], axis=1))
        both = dot(first_ref[...], jnp.concatenate([high, high, low, low], axis=0))
        place(spread, turn_ref, sub, both[:, :SIDE])
        place(spread, turn_ref, sub + 1, both[:, SIDE:])
    spectrum[...] = wide_dot(spread, forward_ref)
    for sub in range(GROUP):
        rows = pl.ds(HALF * sub, HALF)
        sig_r, sig_i = spec_ref[rows, :SIDE], spec_ref[rows, SIDE:]
        filt_r, filt_i = spectrum[rows, :SIDE], spectrum[rows, SIDE:]
        keep(mixed, sub, sig_r * filt_r - sig_i * filt_i, sig_r * filt_i + sig_i * filt_r)
    back[...] = wide_dot(mixed, inverse_ref)
    for sub, value in enumerate(settle(back, last_ref, turn_ref)):
        out_ref[pl.ds(sub, HALF, stride=BACK), :] = value
    total = in_ref[pl.ds(0, HALF), :]
    for source in range(1, 2 * GROUP):
        total = total + in_ref[pl.ds(MID * source, HALF), :]
    out_ref[pl.ds(GROUP, HALF, stride=BACK), :] = total


def finish_kernel(own_ref, in_ref, out_ref, grad_ref):
    def load(odd, row):
        return in_ref[pl.ds(BACK * odd + row, BLOCK, stride=2 * BACK), :]

    conv = jnp.concatenate([load(*divmod(block, GROUP)) for block in range(2 * GROUP)], axis=0)
    out_ref[...] = conv.T.astype(BF)
    odd = own_ref[0] // GROUP
    grad_ref[...] = jnp.where(odd == 0, load(0, GROUP), load(1, GROUP))


def call(kernel, shapes, *args, flops=1000, scratch=(), scalars=0):
    outs = [jax.ShapeDtypeStruct(*one) for one in shapes]
    size = sum(math.prod(a.shape) * a.dtype.itemsize for a in [*args, *outs])
    vmem = pl.BlockSpec(memory_space=pltpu.VMEM)
    specs = [vmem] * len(args)
    specs[:scalars] = [pl.BlockSpec(memory_space=pltpu.SMEM)] * scalars
    result = pl.pallas_call(
        kernel,
        out_shape=outs,
        in_specs=specs,
        out_specs=[vmem] * len(outs),
        scratch_shapes=list(scratch),
        cost_estimate=pl.CostEstimate(flops=flops, bytes_accessed=size, transcendentals=0),
        compiler_params=pltpu.CompilerParams(vmem_limit_bytes=24 * 1024 * 1024),
    )(*args)
    return result if len(shapes) > 1 else result[0]


def exchange(rows, axis, inner):
    parts = lax.axis_size(axis)
    blocks = rows.reshape((parts, *inner, rows.shape[-1]))
    return lax.all_to_all(blocks, axis, split_axis=0, concat_axis=0, tiled=True).reshape(rows.shape)


def body(inputs, cotangent, filter_taps, skip_gain):
    _, rows, chans = inputs.shape
    parts, shares = lax.axis_size("seq"), lax.axis_size("dp")
    own = lax.axis_index("dp").astype(jnp.int32)[None]
    seat = lax.axis_index("seq").astype(jnp.int32)[None]
    wide = 2 * SIDE
    constants = [jnp.asarray(t) for t in tables()]

    def room(count):
        return (
            pltpu.VMEM((count * GROUP * HALF, 2 * wide), BF),
            pltpu.VMEM((count * GROUP * HALF, wide), F32),
            pltpu.VMEM((GROUP * HALF, 2 * wide), BF),
            pltpu.VMEM((GROUP * HALF, wide), F32),
        )

    mask = call(mask_kernel, [((1, chans), F32)], seat, flops=500_000_000, scalars=1)
    packed = call(
        pack_kernel,
        [((SENT * parts, rows), F32)],
        own,
        mask,
        inputs[0],
        cotangent[0],
        filter_taps,
        skip_gain[None],
        scalars=1,
        scratch=(pltpu.VMEM((chans, rows), F32),),
    )
    columns = exchange(packed, "seq", (SENT, 1))
    spec, partial = call(
        grad_kernel,
        [((GROUP * HALF, wide), F32), ((MID * shares, rows), F32)],
        own,
        columns,
        *constants,
        flops=500_000_000,
        scalars=1,
        scratch=(*room(2), pltpu.VMEM((HALF, rows), F32)),
    )
    partial = exchange(partial, "dp", (MID,))
    settled = call(
        conv_kernel,
        [((BACK * parts, rows), F32)],
        partial,
        spec,
        *constants,
        flops=500_000_000,
        scratch=room(1),
    )
    settled = exchange(settled, "seq", (BACK, 1))
    outputs, filter_grad = call(
        finish_kernel,
        [((rows, chans), BF), ((chans // shares, rows), F32)],
        own,
        settled,
        scalars=1,
    )
    return outputs[None], filter_grad.T


def solution(mesh):
    placed = (P("dp", "seq", None), P("dp", "seq", None), P("seq", None), P())
    return jax.shard_map(
        body,
        mesh=mesh,
        in_specs=placed,
        out_specs=(P("dp", "seq", None), P("seq", "dp")),
        check_vma=False,
    )
```

```python
import functools
import math

import jax
import jax.numpy as jnp
import ml_dtypes
import numpy as np
from jax import lax
from jax.experimental import pallas as pl
from jax.experimental.pallas import tpu as pltpu
from jax.sharding import PartitionSpec as P

SIDE = 128
HALF = 64
TOTAL = SIDE * SIDE
GROUP = 4
BLOCK = 32
SENT = 2 * GROUP + 1
BACK = GROUP + 1
MID = HALF + BLOCK
BF = jnp.bfloat16
F32 = jnp.float32


def halves(table):
    high = table.astype(ml_dtypes.bfloat16)
    low = (table - high.astype(np.float64)).astype(ml_dtypes.bfloat16)
    return high, low


def tables():
    blocks = np.arange(HALF)
    places = np.arange(SIDE)
    outer = 2.0 * math.pi * np.outer(np.arange(HALF) + 0.5, blocks) / SIDE
    first = np.concatenate([np.cos(outer), -np.sin(outer)], axis=0)
    high, low = halves(first)
    first_in = np.concatenate([high, low, high, low], axis=1)
    last = first.T * (2.0 / TOTAL)
    high, low = halves(last)
    last_out = np.concatenate([high, high, low], axis=1)
    angle = 2.0 * math.pi * np.outer(np.arange(HALF) + 0.5, places) / TOTAL
    turn = np.stack([np.cos(angle), -np.sin(angle)]).astype(np.float32)
    inner = 2.0 * math.pi * (np.outer(places, places) % SIDE) / SIDE
    cosine, sine = np.cos(inner), np.sin(inner)
    forward = np.block([[cosine, -sine], [sine, cosine]])
    inverse = np.block([[cosine, sine], [-sine, cosine]])
    high, low = halves(forward)
    forward = np.concatenate([high, high, low], axis=0)
    high, low = halves(inverse)
    inverse = np.concatenate([high, high, low], axis=0)
    return first_in, last_out, turn, forward, inverse


def split(value):
    high = value.astype(BF)
    return high, (value - high.astype(F32)).astype(BF)


def dot(left, right):
    return jnp.dot(left, right, preferred_element_type=F32)


def mask_kernel(seat_ref, out_ref):
    out_ref[...] = jnp.where(seat_ref[0] == 0, jnp.ones(out_ref.shape, F32), jnp.zeros(out_ref.shape, F32))


def pack_kernel(own_ref, mask_ref, signal_ref, grads_ref, taps_ref, gain_ref, out_ref, turned):
    for kind, ref in enumerate((signal_ref, grads_ref)):
        value = ref[...].astype(F32).T
        for block in range(2 * GROUP):
            odd, sub = divmod(block, GROUP)
            rows = value[BLOCK * block : BLOCK * (block + 1)]
            out_ref[pl.ds(SENT * odd + GROUP * kind + sub, BLOCK, stride=2 * SENT), :] = rows
    taps = taps_ref[...]
    first = lax.broadcasted_iota(jnp.int32, taps.shape, 0) == 0
    taps = taps + jnp.where(first, gain_ref[...] * mask_ref[...], 0.0)
    turned[...] = taps.T
    sub = own_ref[0] // 2
    for odd in range(2):
        start = pl.multiple_of(BLOCK * (GROUP * odd + sub), BLOCK)
        out_ref[pl.ds(SENT * odd + 2 * GROUP, BLOCK, stride=2 * SENT), :] = turned[pl.ds(start, BLOCK), :]


def place(spread, turn_ref, index, column):
    cosine, sine = turn_ref[0], turn_ref[1]
    real, imag = column[:HALF], column[HALF:]
    real, imag = real * cosine - imag * sine, real * sine + imag * cosine
    keep(spread, index, real, imag)


def keep(ref, index, real, imag):
    rows = pl.ds(HALF * index, HALF)
    for part, value in enumerate((real, imag)):
        high, low = split(value)
        ref[rows, pl.ds(SIDE * part, SIDE)] = high
        ref[rows, pl.ds(2 * SIDE + SIDE * part, SIDE)] = low


def wide_dot(ref, table_ref):
    return dot(ref[...], table_ref[: 4 * SIDE]) + dot(ref[:, : 2 * SIDE], table_ref[4 * SIDE :])


def settle(back, last_ref, turn_ref):
    cosine, sine = turn_ref[0], turn_ref[1]
    stacks = []
    for one in range(GROUP):
        rows = pl.ds(HALF * one, HALF)
        real, imag = back[rows, :SIDE], back[rows, SIDE:]
        value = jnp.concatenate(
            [real * cosine + imag * sine, imag * cosine - real * sine], axis=0
        )
        high, low = split(value)
        stacks.append(jnp.concatenate([high, low, high], axis=0))
    joined = dot(last_ref[...], jnp.concatenate(stacks, axis=1))
    return [joined[:, SIDE * one : SIDE * (one + 1)] for one in range(GROUP)]


def grad_kernel(own_ref, in_ref, first_ref, last_ref, turn_ref, forward_ref, inverse_ref, spec_ref, out_ref, spread, spectrum, mixed, back, taps):
    def load(row):
        return in_ref[pl.ds(row, HALF, stride=SENT), :]

    taps[...] = load(2 * GROUP)
    columns = jnp.concatenate([load(row) for row in range(2 * GROUP)], axis=1).astype(BF)
    joined = dot(first_ref[:, :SIDE], jnp.concatenate([columns, columns], axis=0))
    for index in range(2 * GROUP):
        place(spread, turn_ref, index, joined[:, SIDE * index : SIDE * (index + 1)])
    spectrum[...] = wide_dot(spread, forward_ref)
    spec_ref[...] = spectrum[: GROUP * HALF]
    for sub in range(GROUP):
        parts = []
        for kind in range(2):
            rows = pl.ds(HALF * (GROUP * kind + sub), HALF)
            parts.append((spectrum[rows, :SIDE], spectrum[rows, SIDE:]))
        (sig_r, sig_i), (grad_r, grad_i) = parts
        keep(mixed, sub, grad_r * sig_r + grad_i * sig_i, grad_i * sig_r - grad_r * sig_i)
    back[...] = wide_dot(mixed, inverse_ref)
    for sub, value in enumerate(settle(back, last_ref, turn_ref)):
        for target in range(sub, 2 * GROUP, GROUP):
            out_ref[pl.ds(MID * target, HALF), :] = value
    start = pl.multiple_of(BLOCK * (own_ref[0] % 2), BLOCK)
    half = taps[pl.ds(start, BLOCK), :]
    for target in range(2 * GROUP):
        out_ref[pl.ds(MID * target + HALF, BLOCK), :] = half


def conv_kernel(in_ref, spec_ref, first_ref, last_ref, turn_ref, forward_ref, inverse_ref, out_ref, spread, spectrum, mixed, back):
    def taps(sub):
        starts = [MID * (2 * sub + core) + HALF for core in range(2)]
        return jnp.concatenate([in_ref[pl.ds(start, BLOCK), :] for start in starts], axis=0)

    high, low = split(jnp.concatenate([taps(sub) for sub in range(GROUP)], axis=1))
    joined = dot(first_ref[...], jnp.concatenate([high, high, low, low], axis=0))
    for sub in range(GROUP):
        place(spread, turn_ref, sub, joined[:, SIDE * sub : SIDE * (sub + 1)])
    spectrum[...] = wide_dot(spread, forward_ref)
    for sub in range(GROUP):
        rows = pl.ds(HALF * sub, HALF)
        sig_r, sig_i = spec_ref[rows, :SIDE], spec_ref[rows, SIDE:]
        filt_r, filt_i = spectrum[rows, :SIDE], spectrum[rows, SIDE:]
        keep(mixed, sub, sig_r * filt_r - sig_i * filt_i, sig_r * filt_i + sig_i * filt_r)
    back[...] = wide_dot(mixed, inverse_ref)
    for sub, value in enumerate(settle(back, last_ref, turn_ref)):
        out_ref[pl.ds(sub, HALF, stride=BACK), :] = value
    total = in_ref[pl.ds(0, HALF), :]
    for source in range(1, 2 * GROUP):
        total = total + in_ref[pl.ds(MID * source, HALF), :]
    out_ref[pl.ds(GROUP, HALF, stride=BACK), :] = total


def finish_kernel(own_ref, in_ref, out_ref, grad_ref):
    def load(odd, row):
        return in_ref[pl.ds(BACK * odd + row, BLOCK, stride=2 * BACK), :]

    conv = jnp.concatenate([load(*divmod(block, GROUP)) for block in range(2 * GROUP)], axis=0)
    out_ref[...] = conv.T.astype(BF)
    odd = own_ref[0] // GROUP
    grad_ref[...] = jnp.where(odd == 0, load(0, GROUP), load(1, GROUP))


def call(kernel, shapes, *args, flops=1000, scratch=(), scalars=0):
    outs = [jax.ShapeDtypeStruct(*one) for one in shapes]
    size = sum(math.prod(a.shape) * a.dtype.itemsize for a in [*args, *outs])
    vmem = pl.BlockSpec(memory_space=pltpu.VMEM)
    specs = [vmem] * len(args)
    specs[:scalars] = [pl.BlockSpec(memory_space=pltpu.SMEM)] * scalars
    result = pl.pallas_call(
        kernel,
        out_shape=outs,
        in_specs=specs,
        out_specs=[vmem] * len(outs),
        scratch_shapes=list(scratch),
        cost_estimate=pl.CostEstimate(flops=flops, bytes_accessed=size, transcendentals=0),
        compiler_params=pltpu.CompilerParams(vmem_limit_bytes=24 * 1024 * 1024),
    )(*args)
    return result if len(shapes) > 1 else result[0]


def exchange(rows, axis, inner):
    parts = lax.axis_size(axis)
    blocks = rows.reshape((parts, *inner, rows.shape[-1]))
    return lax.all_to_all(blocks, axis, split_axis=0, concat_axis=0, tiled=True).reshape(rows.shape)


def body(inputs, cotangent, filter_taps, skip_gain):
    _, rows, chans = inputs.shape
    parts, shares = lax.axis_size("seq"), lax.axis_size("dp")
    own = lax.axis_index("dp").astype(jnp.int32)[None]
    seat = lax.axis_index("seq").astype(jnp.int32)[None]
    wide = 2 * SIDE
    constants = [jnp.asarray(t) for t in tables()]

    def room(count):
        return (
            pltpu.VMEM((count * GROUP * HALF, 2 * wide), BF),
            pltpu.VMEM((count * GROUP * HALF, wide), F32),
            pltpu.VMEM((GROUP * HALF, 2 * wide), BF),
            pltpu.VMEM((GROUP * HALF, wide), F32),
        )

    mask = call(mask_kernel, [((1, chans), F32)], seat, flops=500_000_000, scalars=1)
    packed = call(
        pack_kernel,
        [((SENT * parts, rows), F32)],
        own,
        mask,
        inputs[0],
        cotangent[0],
        filter_taps,
        skip_gain[None],
        scalars=1,
        scratch=(pltpu.VMEM((chans, rows), F32),),
    )
    columns = exchange(packed, "seq", (SENT, 1))
    spec, partial = call(
        grad_kernel,
        [((GROUP * HALF, wide), F32), ((MID * shares, rows), F32)],
        own,
        columns,
        *constants,
        flops=500_000_000,
        scalars=1,
        scratch=(*room(2), pltpu.VMEM((HALF, rows), F32)),
    )
    partial = exchange(partial, "dp", (MID,))
    settled = call(
        conv_kernel,
        [((BACK * parts, rows), F32)],
        partial,
        spec,
        *constants,
        flops=500_000_000,
        scratch=room(1),
    )
    settled = exchange(settled, "seq", (BACK, 1))
    outputs, filter_grad = call(
        finish_kernel,
        [((rows, chans), BF), ((chans // shares, rows), F32)],
        own,
        settled,
        scalars=1,
    )
    return outputs[None], filter_grad.T


def solution(mesh):
    placed = (P("dp", "seq", None), P("dp", "seq", None), P("seq", None), P())
    return jax.shard_map(
        body,
        mesh=mesh,
        in_specs=placed,
        out_specs=(P("dp", "seq", None), P("seq", "dp")),
        check_vma=False,
    )
```

```python
import functools
import math

import jax
import jax.numpy as jnp
import ml_dtypes
import numpy as np
from jax import lax
from jax.experimental import pallas as pl
from jax.experimental.pallas import tpu as pltpu
from jax.sharding import PartitionSpec as P

SIDE = 128
HALF = 64
TOTAL = SIDE * SIDE
GROUP = 4
BLOCK = 32
SENT = 2 * GROUP + 1
BACK = GROUP + 1
MID = HALF + BLOCK
BF = jnp.bfloat16
F32 = jnp.float32


def halves(table):
    high = table.astype(ml_dtypes.bfloat16)
    low = (table - high.astype(np.float64)).astype(ml_dtypes.bfloat16)
    return high, low


def tables():
    blocks = np.arange(HALF)
    places = np.arange(SIDE)
    outer = 2.0 * math.pi * np.outer(np.arange(HALF) + 0.5, blocks) / SIDE
    first = np.concatenate([np.cos(outer), -np.sin(outer)], axis=0)
    high, low = halves(first)
    first_in = np.concatenate([high, low, high, low], axis=1)
    last = first.T * (2.0 / TOTAL)
    high, low = halves(last)
    last_out = np.concatenate([high, high, low], axis=1)
    angle = 2.0 * math.pi * np.outer(np.arange(HALF) + 0.5, places) / TOTAL
    turn = np.stack([np.cos(angle), -np.sin(angle)]).astype(np.float32)
    inner = 2.0 * math.pi * (np.outer(places, places) % SIDE) / SIDE
    cosine, sine = np.cos(inner), np.sin(inner)
    forward = np.block([[cosine, -sine], [sine, cosine]])
    inverse = np.block([[cosine, sine], [-sine, cosine]])
    high, low = halves(forward)
    forward = np.concatenate([high, low], axis=0)
    high, low = halves(inverse)
    inverse = np.concatenate([high, low], axis=0)
    return first_in, last_out, turn, forward, inverse


def split(value):
    high = value.astype(BF)
    return high, (value - high.astype(F32)).astype(BF)


def dot(left, right):
    return jnp.dot(left, right, preferred_element_type=F32)


def mask_kernel(seat_ref, out_ref):
    out_ref[...] = jnp.where(seat_ref[0] == 0, jnp.ones(out_ref.shape, F32), jnp.zeros(out_ref.shape, F32))


def pack_kernel(own_ref, mask_ref, signal_ref, grads_ref, taps_ref, gain_ref, out_ref, turned):
    for kind, ref in enumerate((signal_ref, grads_ref)):
        value = ref[...].astype(F32).T
        for block in range(2 * GROUP):
            odd, sub = divmod(block, GROUP)
            rows = value[BLOCK * block : BLOCK * (block + 1)]
            out_ref[pl.ds(SENT * odd + GROUP * kind + sub, BLOCK, stride=2 * SENT), :] = rows
    taps = taps_ref[...]
    first = lax.broadcasted_iota(jnp.int32, taps.shape, 0) == 0
    taps = taps + jnp.where(first, gain_ref[...] * mask_ref[...], 0.0)
    turned[...] = taps.T
    sub = own_ref[0] // 2
    for odd in range(2):
        start = pl.multiple_of(BLOCK * (GROUP * odd + sub), BLOCK)
        out_ref[pl.ds(SENT * odd + 2 * GROUP, BLOCK, stride=2 * SENT), :] = turned[pl.ds(start, BLOCK), :]


def place(spread, turn_ref, index, column):
    cosine, sine = turn_ref[0], turn_ref[1]
    real, imag = column[:HALF], column[HALF:]
    real, imag = real * cosine - imag * sine, real * sine + imag * cosine
    keep(spread, index, real, imag)


def keep(ref, index, real, imag):
    count = ref.shape[0] // 2
    for part, value in enumerate((real, imag)):
        high, low = split(value)
        lanes = pl.ds(SIDE * part, SIDE)
        ref[pl.ds(HALF * index, HALF), lanes] = high
        ref[pl.ds(count + HALF * index, HALF), lanes] = low


def wide_dot(ref, table_ref):
    count = ref.shape[0] // 2
    joined = dot(ref[...], table_ref[: 2 * SIDE])
    return joined[:count] + joined[count:] + dot(ref[:count], table_ref[2 * SIDE :])


def settle(back, last_ref, turn_ref):
    cosine, sine = turn_ref[0], turn_ref[1]
    stacks = []
    for one in range(GROUP):
        rows = pl.ds(HALF * one, HALF)
        real, imag = back[rows, :SIDE], back[rows, SIDE:]
        value = jnp.concatenate(
            [real * cosine + imag * sine, imag * cosine - real * sine], axis=0
        )
        high, low = split(value)
        stacks.append(jnp.concatenate([high, low, high], axis=0))
    joined = dot(last_ref[...], jnp.concatenate(stacks, axis=1))
    return [joined[:, SIDE * one : SIDE * (one + 1)] for one in range(GROUP)]


def grad_kernel(own_ref, in_ref, first_ref, last_ref, turn_ref, forward_ref, inverse_ref, spec_ref, out_ref, spread, spectrum, mixed, back, taps):
    def load(row):
        return in_ref[pl.ds(row, HALF, stride=SENT), :]

    taps[...] = load(2 * GROUP)
    columns = jnp.concatenate([load(row) for row in range(2 * GROUP)], axis=1).astype(BF)
    joined = dot(first_ref[:, :SIDE], jnp.concatenate([columns, columns], axis=0))
    for index in range(2 * GROUP):
        place(spread, turn_ref, index, joined[:, SIDE * index : SIDE * (index + 1)])
    spectrum[...] = wide_dot(spread, forward_ref)
    spec_ref[...] = spectrum[: GROUP * HALF]
    for sub in range(GROUP):
        parts = []
        for kind in range(2):
            rows = pl.ds(HALF * (GROUP * kind + sub), HALF)
            parts.append((spectrum[rows, :SIDE], spectrum[rows, SIDE:]))
        (sig_r, sig_i), (grad_r, grad_i) = parts
        keep(mixed, sub, grad_r * sig_r + grad_i * sig_i, grad_i * sig_r - grad_r * sig_i)
    back[...] = wide_dot(mixed, inverse_ref)
    for sub, value in enumerate(settle(back, last_ref, turn_ref)):
        for target in range(sub, 2 * GROUP, GROUP):
            out_ref[pl.ds(MID * target, HALF), :] = value
    start = pl.multiple_of(BLOCK * (own_ref[0] % 2), BLOCK)
    half = taps[pl.ds(start, BLOCK), :]
    for target in range(2 * GROUP):
        out_ref[pl.ds(MID * target + HALF, BLOCK), :] = half


def conv_kernel(in_ref, spec_ref, first_ref, last_ref, turn_ref, forward_ref, inverse_ref, out_ref, spread, spectrum, mixed, back):
    def taps(sub):
        starts = [MID * (2 * sub + core) + HALF for core in range(2)]
        return jnp.concatenate([in_ref[pl.ds(start, BLOCK), :] for start in starts], axis=0)

    high, low = split(jnp.concatenate([taps(sub) for sub in range(GROUP)], axis=1))
    joined = dot(first_ref[...], jnp.concatenate([high, high, low, low], axis=0))
    for sub in range(GROUP):
        place(spread, turn_ref, sub, joined[:, SIDE * sub : SIDE * (sub + 1)])
    spectrum[...] = wide_dot(spread, forward_ref)
    for sub in range(GROUP):
        rows = pl.ds(HALF * sub, HALF)
        sig_r, sig_i = spec_ref[rows, :SIDE], spec_ref[rows, SIDE:]
        filt_r, filt_i = spectrum[rows, :SIDE], spectrum[rows, SIDE:]
        keep(mixed, sub, sig_r * filt_r - sig_i * filt_i, sig_r * filt_i + sig_i * filt_r)
    back[...] = wide_dot(mixed, inverse_ref)
    for sub, value in enumerate(settle(back, last_ref, turn_ref)):
        out_ref[pl.ds(sub, HALF, stride=BACK), :] = value
    total = in_ref[pl.ds(0, HALF), :]
    for source in range(1, 2 * GROUP):
        total = total + in_ref[pl.ds(MID * source, HALF), :]
    out_ref[pl.ds(GROUP, HALF, stride=BACK), :] = total


def finish_kernel(own_ref, in_ref, out_ref, grad_ref):
    def load(odd, row):
        return in_ref[pl.ds(BACK * odd + row, BLOCK, stride=2 * BACK), :]

    conv = jnp.concatenate([load(*divmod(block, GROUP)) for block in range(2 * GROUP)], axis=0)
    out_ref[...] = conv.T.astype(BF)
    odd = own_ref[0] // GROUP
    grad_ref[...] = jnp.where(odd == 0, load(0, GROUP), load(1, GROUP))


def call(kernel, shapes, *args, flops=1000, scratch=(), scalars=0):
    outs = [jax.ShapeDtypeStruct(*one) for one in shapes]
    size = sum(math.prod(a.shape) * a.dtype.itemsize for a in [*args, *outs])
    vmem = pl.BlockSpec(memory_space=pltpu.VMEM)
    specs = [vmem] * len(args)
    specs[:scalars] = [pl.BlockSpec(memory_space=pltpu.SMEM)] * scalars
    result = pl.pallas_call(
        kernel,
        out_shape=outs,
        in_specs=specs,
        out_specs=[vmem] * len(outs),
        scratch_shapes=list(scratch),
        cost_estimate=pl.CostEstimate(flops=flops, bytes_accessed=size, transcendentals=0),
        compiler_params=pltpu.CompilerParams(vmem_limit_bytes=24 * 1024 * 1024),
    )(*args)
    return result if len(shapes) > 1 else result[0]


def exchange(rows, axis, inner):
    parts = lax.axis_size(axis)
    blocks = rows.reshape((parts, *inner, rows.shape[-1]))
    return lax.all_to_all(blocks, axis, split_axis=0, concat_axis=0, tiled=True).reshape(rows.shape)


def body(inputs, cotangent, filter_taps, skip_gain):
    _, rows, chans = inputs.shape
    parts, shares = lax.axis_size("seq"), lax.axis_size("dp")
    own = lax.axis_index("dp").astype(jnp.int32)[None]
    seat = lax.axis_index("seq").astype(jnp.int32)[None]
    wide = 2 * SIDE
    constants = [jnp.asarray(t) for t in tables()]

    def room(count):
        return (
            pltpu.VMEM((2 * count * GROUP * HALF, wide), BF),
            pltpu.VMEM((count * GROUP * HALF, wide), F32),
            pltpu.VMEM((2 * GROUP * HALF, wide), BF),
            pltpu.VMEM((GROUP * HALF, wide), F32),
        )

    mask = call(mask_kernel, [((1, chans), F32)], seat, flops=500_000_000, scalars=1)
    packed = call(
        pack_kernel,
        [((SENT * parts, rows), F32)],
        own,
        mask,
        inputs[0],
        cotangent[0],
        filter_taps,
        skip_gain[None],
        scalars=1,
        scratch=(pltpu.VMEM((chans, rows), F32),),
    )
    columns = exchange(packed, "seq", (SENT, 1))
    spec, partial = call(
        grad_kernel,
        [((GROUP * HALF, wide), F32), ((MID * shares, rows), F32)],
        own,
        columns,
        *constants,
        flops=500_000_000,
        scalars=1,
        scratch=(*room(2), pltpu.VMEM((HALF, rows), F32)),
    )
    partial = exchange(partial, "dp", (MID,))
    settled = call(
        conv_kernel,
        [((BACK * parts, rows), F32)],
        partial,
        spec,
        *constants,
        flops=500_000_000,
        scratch=room(1),
    )
    settled = exchange(settled, "seq", (BACK, 1))
    outputs, filter_grad = call(
        finish_kernel,
        [((rows, chans), BF), ((chans // shares, rows), F32)],
        own,
        settled,
        scalars=1,
    )
    return outputs[None], filter_grad.T


def solution(mesh):
    placed = (P("dp", "seq", None), P("dp", "seq", None), P("seq", None), P())
    return jax.shard_map(
        body,
        mesh=mesh,
        in_specs=placed,
        out_specs=(P("dp", "seq", None), P("seq", "dp")),
        check_vma=False,
    )
```

```python
import functools
import math

import jax
import jax.numpy as jnp
import ml_dtypes
import numpy as np
from jax import lax
from jax.experimental import pallas as pl
from jax.experimental.pallas import tpu as pltpu
from jax.sharding import PartitionSpec as P

SIDE = 128
HALF = 64
TOTAL = SIDE * SIDE
GROUP = 4
BLOCK = 32
SENT = 2 * GROUP + 1
BACK = GROUP + 1
MID = HALF + BLOCK
BF = jnp.bfloat16
F32 = jnp.float32


def halves(table):
    high = table.astype(ml_dtypes.bfloat16)
    low = (table - high.astype(np.float64)).astype(ml_dtypes.bfloat16)
    return high, low


def tables():
    blocks = np.arange(HALF)
    places = np.arange(SIDE)
    outer = 2.0 * math.pi * np.outer(np.arange(HALF) + 0.5, blocks) / SIDE
    first = np.concatenate([np.cos(outer), -np.sin(outer)], axis=0)
    high, low = halves(first)
    first_in = np.concatenate([high, low, high, low], axis=1)
    last = first.T * (2.0 / TOTAL)
    high, low = halves(last)
    last_out = np.concatenate([high, high, low], axis=1)
    angle = 2.0 * math.pi * np.outer(np.arange(HALF) + 0.5, places) / TOTAL
    turn = np.stack([np.cos(angle), -np.sin(angle)]).astype(np.float32)
    inner = 2.0 * math.pi * (np.outer(places, places) % SIDE) / SIDE
    cosine, sine = np.cos(inner), np.sin(inner)
    forward = np.block([[cosine, -sine], [sine, cosine]])
    inverse = np.block([[cosine, sine], [-sine, cosine]])
    high, low = halves(forward)
    forward = np.concatenate([high, low], axis=0)
    high, low = halves(inverse)
    inverse = np.concatenate([high, low], axis=0)
    return first_in, last_out, turn, forward, inverse


def split(value):
    high = value.astype(BF)
    return high, (value - high.astype(F32)).astype(BF)


def dot(left, right):
    return jnp.dot(left, right, preferred_element_type=F32)


def mask_kernel(seat_ref, out_ref):
    out_ref[...] = jnp.where(seat_ref[0] == 0, jnp.ones(out_ref.shape, F32), jnp.zeros(out_ref.shape, F32))


def pack_kernel(own_ref, mask_ref, signal_ref, grads_ref, taps_ref, gain_ref, out_ref, turned):
    for kind, ref in enumerate((signal_ref, grads_ref)):
        value = ref[...].astype(F32).T
        for block in range(2 * GROUP):
            odd, sub = divmod(block, GROUP)
            rows = value[BLOCK * block : BLOCK * (block + 1)]
            out_ref[pl.ds(SENT * odd + GROUP * kind + sub, BLOCK, stride=2 * SENT), :] = rows
    taps = taps_ref[...]
    first = lax.broadcasted_iota(jnp.int32, taps.shape, 0) == 0
    taps = taps + jnp.where(first, gain_ref[...] * mask_ref[...], 0.0)
    turned[...] = taps.T
    sub = own_ref[0] // 2
    for odd in range(2):
        start = pl.multiple_of(BLOCK * (GROUP * odd + sub), BLOCK)
        out_ref[pl.ds(SENT * odd + 2 * GROUP, BLOCK, stride=2 * SENT), :] = turned[pl.ds(start, BLOCK), :]


def place(spread, turn_ref, index, column):
    cosine, sine = turn_ref[0], turn_ref[1]
    real, imag = column[:HALF], column[HALF:]
    real, imag = real * cosine - imag * sine, real * sine + imag * cosine
    keep(spread, index, real, imag)


def keep(ref, index, real, imag):
    count = ref.shape[0] // 2
    for part, value in enumerate((real, imag)):
        high, low = split(value)
        lanes = pl.ds(SIDE * part, SIDE)
        ref[pl.ds(HALF * index, HALF), lanes] = high
        ref[pl.ds(count + HALF * index, HALF), lanes] = low


def wide_dot(ref, table_ref):
    count = ref.shape[0] // 2
    joined = dot(ref[...], table_ref[: 2 * SIDE])
    return joined[:count] + joined[count:] + dot(ref[:count], table_ref[2 * SIDE :])


def settle(back, last_ref, turn_ref):
    cosine, sine = turn_ref[0], turn_ref[1]
    stacks = []
    for one in range(GROUP):
        rows = pl.ds(HALF * one, HALF)
        real, imag = back[rows, :SIDE], back[rows, SIDE:]
        value = jnp.concatenate(
            [real * cosine + imag * sine, imag * cosine - real * sine], axis=0
        )
        high, low = split(value)
        stacks.append(jnp.concatenate([high, low, high], axis=0))
    joined = dot(last_ref[...], jnp.concatenate(stacks, axis=1))
    return [joined[:, SIDE * one : SIDE * (one + 1)] for one in range(GROUP)]


def grad_kernel(own_ref, in_ref, first_ref, last_ref, turn_ref, forward_ref, inverse_ref, spec_ref, out_ref, spread, spectrum, mixed, back, taps):
    def load(row):
        return in_ref[pl.ds(row, HALF, stride=SENT), :]

    taps[...] = load(2 * GROUP)
    start = pl.multiple_of(BLOCK * (own_ref[0] % 2), BLOCK)
    half = taps[pl.ds(start, BLOCK), :]
    for target in range(2 * GROUP):
        out_ref[pl.ds(MID * target + HALF, BLOCK), :] = half
    columns = jnp.concatenate([load(row) for row in range(2 * GROUP)], axis=1).astype(BF)
    joined = dot(first_ref[:, :SIDE], jnp.concatenate([columns, columns], axis=0))
    for index in range(2 * GROUP):
        place(spread, turn_ref, index, joined[:, SIDE * index : SIDE * (index + 1)])
    spectrum[...] = wide_dot(spread, forward_ref)
    spec_ref[...] = spectrum[: GROUP * HALF]
    for sub in range(GROUP):
        parts = []
        for kind in range(2):
            rows = pl.ds(HALF * (GROUP * kind + sub), HALF)
            parts.append((spectrum[rows, :SIDE], spectrum[rows, SIDE:]))
        (sig_r, sig_i), (grad_r, grad_i) = parts
        keep(mixed, sub, grad_r * sig_r + grad_i * sig_i, grad_i * sig_r - grad_r * sig_i)
    back[...] = wide_dot(mixed, inverse_ref)
    for sub, value in enumerate(settle(back, last_ref, turn_ref)):
        for target in range(sub, 2 * GROUP, GROUP):
            out_ref[pl.ds(MID * target, HALF), :] = value


def conv_kernel(in_ref, spec_ref, first_ref, last_ref, turn_ref, forward_ref, inverse_ref, out_ref, spread, spectrum, mixed, back):
    def taps(sub):
        starts = [MID * (2 * sub + core) + HALF for core in range(2)]
        return jnp.concatenate([in_ref[pl.ds(start, BLOCK), :] for start in starts], axis=0)

    total = in_ref[pl.ds(0, HALF), :]
    for source in range(1, 2 * GROUP):
        total = total + in_ref[pl.ds(MID * source, HALF), :]
    out_ref[pl.ds(GROUP, HALF, stride=BACK), :] = total
    high, low = split(jnp.concatenate([taps(sub) for sub in range(GROUP)], axis=1))
    joined = dot(first_ref[...], jnp.concatenate([high, high, low, low], axis=0))
    for sub in range(GROUP):
        place(spread, turn_ref, sub, joined[:, SIDE * sub : SIDE * (sub + 1)])
    spectrum[...] = wide_dot(spread, forward_ref)
    for sub in range(GROUP):
        rows = pl.ds(HALF * sub, HALF)
        sig_r, sig_i = spec_ref[rows, :SIDE], spec_ref[rows, SIDE:]
        filt_r, filt_i = spectrum[rows, :SIDE], spectrum[rows, SIDE:]
        keep(mixed, sub, sig_r * filt_r - sig_i * filt_i, sig_r * filt_i + sig_i * filt_r)
    back[...] = wide_dot(mixed, inverse_ref)
    for sub, value in enumerate(settle(back, last_ref, turn_ref)):
        out_ref[pl.ds(sub, HALF, stride=BACK), :] = value


def finish_kernel(own_ref, in_ref, out_ref, grad_ref):
    def load(odd, row):
        return in_ref[pl.ds(BACK * odd + row, BLOCK, stride=2 * BACK), :]

    conv = jnp.concatenate([load(*divmod(block, GROUP)) for block in range(2 * GROUP)], axis=0)
    out_ref[...] = conv.T.astype(BF)
    odd = own_ref[0] // GROUP
    grad_ref[...] = jnp.where(odd == 0, load(0, GROUP), load(1, GROUP))


def call(kernel, shapes, *args, flops=1000, scratch=(), scalars=0):
    outs = [jax.ShapeDtypeStruct(*one) for one in shapes]
    size = sum(math.prod(a.shape) * a.dtype.itemsize for a in [*args, *outs])
    vmem = pl.BlockSpec(memory_space=pltpu.VMEM)
    specs = [vmem] * len(args)
    specs[:scalars] = [pl.BlockSpec(memory_space=pltpu.SMEM)] * scalars
    result = pl.pallas_call(
        kernel,
        out_shape=outs,
        in_specs=specs,
        out_specs=[vmem] * len(outs),
        scratch_shapes=list(scratch),
        cost_estimate=pl.CostEstimate(flops=flops, bytes_accessed=size, transcendentals=0),
        compiler_params=pltpu.CompilerParams(vmem_limit_bytes=24 * 1024 * 1024),
    )(*args)
    return result if len(shapes) > 1 else result[0]


def exchange(rows, axis, inner):
    parts = lax.axis_size(axis)
    blocks = rows.reshape((parts, *inner, rows.shape[-1]))
    return lax.all_to_all(blocks, axis, split_axis=0, concat_axis=0, tiled=True).reshape(rows.shape)


def body(inputs, cotangent, filter_taps, skip_gain):
    _, rows, chans = inputs.shape
    parts, shares = lax.axis_size("seq"), lax.axis_size("dp")
    own = lax.axis_index("dp").astype(jnp.int32)[None]
    seat = lax.axis_index("seq").astype(jnp.int32)[None]
    wide = 2 * SIDE
    constants = [jnp.asarray(t) for t in tables()]

    def room(count):
        return (
            pltpu.VMEM((2 * count * GROUP * HALF, wide), BF),
            pltpu.VMEM((count * GROUP * HALF, wide), F32),
            pltpu.VMEM((2 * GROUP * HALF, wide), BF),
            pltpu.VMEM((GROUP * HALF, wide), F32),
        )

    mask = call(mask_kernel, [((1, chans), F32)], seat, flops=500_000_000, scalars=1)
    packed = call(
        pack_kernel,
        [((SENT * parts, rows), F32)],
        own,
        mask,
        inputs[0],
        cotangent[0],
        filter_taps,
        skip_gain[None],
        scalars=1,
        scratch=(pltpu.VMEM((chans, rows), F32),),
    )
    columns = exchange(packed, "seq", (SENT, 1))
    spec, partial = call(
        grad_kernel,
        [((GROUP * HALF, wide), F32), ((MID * shares, rows), F32)],
        own,
        columns,
        *constants,
        flops=500_000_000,
        scalars=1,
        scratch=(*room(2), pltpu.VMEM((HALF, rows), F32)),
    )
    partial = exchange(partial, "dp", (MID,))
    settled = call(
        conv_kernel,
        [((BACK * parts, rows), F32)],
        partial,
        spec,
        *constants,
        flops=500_000_000,
        scratch=room(1),
    )
    settled = exchange(settled, "seq", (BACK, 1))
    outputs, filter_grad = call(
        finish_kernel,
        [((rows, chans), BF), ((chans // shares, rows), F32)],
        own,
        settled,
        scalars=1,
    )
    return outputs[None], filter_grad.T


def solution(mesh):
    placed = (P("dp", "seq", None), P("dp", "seq", None), P("seq", None), P())
    return jax.shard_map(
        body,
        mesh=mesh,
        in_specs=placed,
        out_specs=(P("dp", "seq", None), P("seq", "dp")),
        check_vma=False,
    )
```

```python
import functools
import math

import jax
import jax.numpy as jnp
import ml_dtypes
import numpy as np
from jax import lax
from jax.experimental import pallas as pl
from jax.experimental.pallas import tpu as pltpu
from jax.sharding import PartitionSpec as P

SIDE = 128
HALF = 64
TOTAL = SIDE * SIDE
GROUP = 4
BLOCK = 32
SENT = 2 * GROUP + 1
BACK = GROUP + 1
MID = HALF + BLOCK
BF = jnp.bfloat16
F32 = jnp.float32


def halves(table):
    high = table.astype(ml_dtypes.bfloat16)
    low = (table - high.astype(np.float64)).astype(ml_dtypes.bfloat16)
    return high, low


def tables():
    blocks = np.arange(HALF)
    places = np.arange(SIDE)
    outer = 2.0 * math.pi * np.outer(np.arange(HALF) + 0.5, blocks) / SIDE
    first = np.concatenate([np.cos(outer), -np.sin(outer)], axis=0)
    high, low = halves(first)
    first_in = np.concatenate([high, low, high, low], axis=1)
    last = first.T * (2.0 / TOTAL)
    high, low = halves(last)
    last_out = np.concatenate([high, high, low], axis=1)
    angle = 2.0 * math.pi * np.outer(np.arange(HALF) + 0.5, places) / TOTAL
    turn = np.stack([np.cos(angle), -np.sin(angle)]).astype(np.float32)
    inner = 2.0 * math.pi * (np.outer(places, places) % SIDE) / SIDE
    cosine, sine = np.cos(inner), np.sin(inner)
    forward = np.block([[cosine, -sine], [sine, cosine]])
    inverse = np.block([[cosine, sine], [-sine, cosine]])
    high, low = halves(forward)
    forward = np.concatenate([high, low], axis=0)
    high, low = halves(inverse)
    inverse = np.concatenate([high, low], axis=0)
    return first_in, last_out, turn, forward, inverse


def split(value):
    high = value.astype(BF)
    return high, (value - high.astype(F32)).astype(BF)


def dot(left, right):
    return jnp.dot(left, right, preferred_element_type=F32)


def mask_kernel(seat_ref, out_ref):
    out_ref[...] = jnp.where(seat_ref[0] == 0, jnp.ones(out_ref.shape, F32), jnp.zeros(out_ref.shape, F32))


def pack_kernel(own_ref, mask_ref, signal_ref, grads_ref, taps_ref, gain_ref, out_ref, turned):
    for kind, ref in enumerate((signal_ref, grads_ref)):
        value = ref[...].astype(F32).T
        for block in range(2 * GROUP):
            odd, sub = divmod(block, GROUP)
            rows = value[BLOCK * block : BLOCK * (block + 1)]
            out_ref[pl.ds(SENT * odd + GROUP * kind + sub, BLOCK, stride=2 * SENT), :] = rows
    taps = taps_ref[...]
    first = lax.broadcasted_iota(jnp.int32, taps.shape, 0) == 0
    taps = taps + jnp.where(first, gain_ref[...] * mask_ref[...], 0.0)
    turned[...] = taps.T
    sub = own_ref[0] // 2
    for odd in range(2):
        start = pl.multiple_of(BLOCK * (GROUP * odd + sub), BLOCK)
        out_ref[pl.ds(SENT * odd + 2 * GROUP, BLOCK, stride=2 * SENT), :] = turned[pl.ds(start, BLOCK), :]


def place(spread, turn_ref, index, column):
    cosine, sine = turn_ref[0], turn_ref[1]
    real, imag = column[:HALF], column[HALF:]
    real, imag = real * cosine - imag * sine, real * sine + imag * cosine
    keep(spread, index, real, imag)


def keep(ref, index, real, imag):
    count = ref.shape[0] // 2
    for part, value in enumerate((real, imag)):
        high, low = split(value)
        lanes = pl.ds(SIDE * part, SIDE)
        ref[pl.ds(HALF * index, HALF), lanes] = high
        ref[pl.ds(count + HALF * index, HALF), lanes] = low


def wide_dot(ref, table_ref):
    count = ref.shape[0] // 2
    joined = dot(ref[...], table_ref[: 2 * SIDE])
    return joined[:count] + joined[count:] + dot(ref[:count], table_ref[2 * SIDE :])


def settle(back, last_ref, turn_ref):
    cosine, sine = turn_ref[0], turn_ref[1]
    stacks = []
    for one in range(GROUP):
        rows = pl.ds(HALF * one, HALF)
        real, imag = back[rows, :SIDE], back[rows, SIDE:]
        value = jnp.concatenate(
            [real * cosine + imag * sine, imag * cosine - real * sine], axis=0
        )
        high, low = split(value)
        stacks.append(jnp.concatenate([high, low, high], axis=0))
    joined = dot(last_ref[...], jnp.concatenate(stacks, axis=1))
    return [joined[:, SIDE * one : SIDE * (one + 1)] for one in range(GROUP)]


def grad_kernel(own_ref, in_ref, first_ref, last_ref, turn_ref, forward_ref, inverse_ref, spec_ref, out_ref, spread, spectrum, mixed, back, taps):
    def load(row):
        return in_ref[pl.ds(row, HALF, stride=SENT), :]

    taps[...] = load(2 * GROUP)
    columns = jnp.concatenate([load(row) for row in range(2 * GROUP)], axis=1).astype(BF)
    joined = dot(first_ref[:, :SIDE], jnp.concatenate([columns, columns], axis=0))
    for index in range(2 * GROUP):
        place(spread, turn_ref, index, joined[:, SIDE * index : SIDE * (index + 1)])
    spectrum[...] = wide_dot(spread, forward_ref)
    spec_ref[...] = spectrum[: GROUP * HALF]
    for sub in range(GROUP):
        parts = []
        for kind in range(2):
            rows = pl.ds(HALF * (GROUP * kind + sub), HALF)
            parts.append((spectrum[rows, :SIDE], spectrum[rows, SIDE:]))
        (sig_r, sig_i), (grad_r, grad_i) = parts
        keep(mixed, sub, grad_r * sig_r + grad_i * sig_i, grad_i * sig_r - grad_r * sig_i)
    back[...] = wide_dot(mixed, inverse_ref)
    for sub, value in enumerate(settle(back, last_ref, turn_ref)):
        for target in range(sub, 2 * GROUP, GROUP):
            out_ref[pl.ds(MID * target, HALF), :] = value
    start = pl.multiple_of(BLOCK * (own_ref[0] % 2), BLOCK)
    half = taps[pl.ds(start, BLOCK), :]
    for target in range(2 * GROUP):
        out_ref[pl.ds(MID * target + HALF, BLOCK), :] = half


def conv_kernel(in_ref, spec_ref, first_ref, last_ref, turn_ref, forward_ref, inverse_ref, out_ref, spread, spectrum, mixed, back):
    def taps(sub):
        starts = [MID * (2 * sub + core) + HALF for core in range(2)]
        return jnp.concatenate([in_ref[pl.ds(start, BLOCK), :] for start in starts], axis=0)

    total = in_ref[pl.ds(0, HALF), :]
    for source in range(1, 2 * GROUP):
        total = total + in_ref[pl.ds(MID * source, HALF), :]
    out_ref[pl.ds(GROUP, HALF, stride=BACK), :] = total
    high, low = split(jnp.concatenate([taps(sub) for sub in range(GROUP)], axis=1))
    joined = dot(first_ref[...], jnp.concatenate([high, high, low, low], axis=0))
    for sub in range(GROUP):
        place(spread, turn_ref, sub, joined[:, SIDE * sub : SIDE * (sub + 1)])
    spectrum[...] = wide_dot(spread, forward_ref)
    for sub in range(GROUP):
        rows = pl.ds(HALF * sub, HALF)
        sig_r, sig_i = spec_ref[rows, :SIDE], spec_ref[rows, SIDE:]
        filt_r, filt_i = spectrum[rows, :SIDE], spectrum[rows, SIDE:]
        keep(mixed, sub, sig_r * filt_r - sig_i * filt_i, sig_r * filt_i + sig_i * filt_r)
    back[...] = wide_dot(mixed, inverse_ref)
    for sub, value in enumerate(settle(back, last_ref, turn_ref)):
        out_ref[pl.ds(sub, HALF, stride=BACK), :] = value


def finish_kernel(own_ref, in_ref, out_ref, grad_ref):
    def load(odd, row):
        return in_ref[pl.ds(BACK * odd + row, BLOCK, stride=2 * BACK), :]

    conv = jnp.concatenate([load(*divmod(block, GROUP)) for block in range(2 * GROUP)], axis=0)
    out_ref[...] = conv.T.astype(BF)
    odd = own_ref[0] // GROUP
    grad_ref[...] = jnp.where(odd == 0, load(0, GROUP), load(1, GROUP))


def call(kernel, shapes, *args, flops=1000, scratch=(), scalars=0):
    outs = [jax.ShapeDtypeStruct(*one) for one in shapes]
    size = sum(math.prod(a.shape) * a.dtype.itemsize for a in [*args, *outs])
    vmem = pl.BlockSpec(memory_space=pltpu.VMEM)
    specs = [vmem] * len(args)
    specs[:scalars] = [pl.BlockSpec(memory_space=pltpu.SMEM)] * scalars
    result = pl.pallas_call(
        kernel,
        out_shape=outs,
        in_specs=specs,
        out_specs=[vmem] * len(outs),
        scratch_shapes=list(scratch),
        cost_estimate=pl.CostEstimate(flops=flops, bytes_accessed=size, transcendentals=0),
        compiler_params=pltpu.CompilerParams(vmem_limit_bytes=24 * 1024 * 1024),
    )(*args)
    return result if len(shapes) > 1 else result[0]


def exchange(rows, axis, inner):
    parts = lax.axis_size(axis)
    blocks = rows.reshape((parts, *inner, rows.shape[-1]))
    return lax.all_to_all(blocks, axis, split_axis=0, concat_axis=0, tiled=True).reshape(rows.shape)


def body(inputs, cotangent, filter_taps, skip_gain):
    _, rows, chans = inputs.shape
    parts, shares = lax.axis_size("seq"), lax.axis_size("dp")
    own = lax.axis_index("dp").astype(jnp.int32)[None]
    seat = lax.axis_index("seq").astype(jnp.int32)[None]
    wide = 2 * SIDE
    constants = [jnp.asarray(t) for t in tables()]

    def room(count):
        return (
            pltpu.VMEM((2 * count * GROUP * HALF, wide), BF),
            pltpu.VMEM((count * GROUP * HALF, wide), F32),
            pltpu.VMEM((2 * GROUP * HALF, wide), BF),
            pltpu.VMEM((GROUP * HALF, wide), F32),
        )

    mask = call(mask_kernel, [((1, chans), F32)], seat, flops=500_000_000, scalars=1)
    packed = call(
        pack_kernel,
        [((SENT * parts, rows), F32)],
        own,
        mask,
        inputs[0],
        cotangent[0],
        filter_taps,
        skip_gain[None],
        scalars=1,
        scratch=(pltpu.VMEM((chans, rows), F32),),
    )
    columns = exchange(packed, "seq", (SENT, 1))
    spec, partial = call(
        grad_kernel,
        [((GROUP * HALF, wide), F32), ((MID * shares, rows), F32)],
        own,
        columns,
        *constants,
        flops=500_000_000,
        scalars=1,
        scratch=(*room(2), pltpu.VMEM((HALF, rows), F32)),
    )
    partial = exchange(partial, "dp", (MID,))
    settled = call(
        conv_kernel,
        [((BACK * parts, rows), F32)],
        partial,
        spec,
        *constants,
        flops=500_000_000,
        scratch=room(1),
    )
    settled = exchange(settled, "seq", (BACK, 1))
    outputs, filter_grad = call(
        finish_kernel,
        [((rows, chans), BF), ((chans // shares, rows), F32)],
        own,
        settled,
        scalars=1,
    )
    return outputs[None], filter_grad.T


def solution(mesh):
    placed = (P("dp", "seq", None), P("dp", "seq", None), P("seq", None), P())
    return jax.shard_map(
        body,
        mesh=mesh,
        in_specs=placed,
        out_specs=(P("dp", "seq", None), P("seq", "dp")),
        check_vma=False,
    )
```
